32 devices in a mesh: samp: 8 (over z, core), par: 4 (over y, x).
Axes of the slice: x: 2, y: 2, z: 4, core: 2. Of those that a mesh axis runs over, the one named last changes fastest.
Arguments:
- activations: bfloat16 [128, 2, 64, 256], P('samp'), may hold values from 0 to 2
- cotangents: bfloat16 [128, 2, 64, 256], P('samp', None, 'par'), may hold values from -0.029907227 to 0.099609375
- energies: float32 [128], P('samp'), may hold values from -3 to -1
Outputs:
- update: float32 [64, 1152], P('par')
- coeffs: float32 [128], P('samp')
The draws below stay inside these ranges and needn't reach their ends.
All inputs are finite; a program needn't handle non-finite values.
Results may differ from the reference program's by a relative error of at most 0.0034.
Values may be sent and summed in bfloat16 or wider, within the bound.
No kernel may reach another device: no remote copies, remote signals or barrier semaphores. Data moves between devices by JAX's collectives and lax.ppermute only.
A program may use at most 128 MiB of HBM per device.

```python
import math
import jax
import jax.numpy as jnp
from jax import lax

C = 64
SIDE = 16
LAYERS = 2
SITES = 256
SAMPLES = 128
N_SAMP = 8


def levels(rng, extent, shards, low, high):
    level, own = 1.0, jax.random.fold_in(rng, 6)
    for position, blocks in shards:
        heights = jnp.exp(jax.random.uniform(jax.random.fold_in(own, position), (blocks,), jnp.float32, low / len(shards), high / len(shards)))
        level = level * jnp.repeat(heights, extent[position] // blocks).reshape([-1 if axis == position else 1 for axis in range(len(extent))])
    return level


def setup_inputs(seed: int = 0) -> dict:
    splits = jax.random.split(jax.random.key(seed), 4)
    activations = jnp.clip(2.0 * jax.random.uniform(splits[0], (SAMPLES, LAYERS, C, SITES), jnp.float32) ** levels(splits[0], (SAMPLES, LAYERS, C, SITES), ((0, 8),), -0.2, 0.2), 0.0, 2.0).astype(jnp.bfloat16)
    cotangents = jnp.clip(-0.029907227 + 0.1295166 * jax.random.uniform(splits[1], (SAMPLES, LAYERS, C, SITES), jnp.float32) ** levels(splits[1], (SAMPLES, LAYERS, C, SITES), ((0, 8), (2, 4)), -0.2, 0.2), -0.029907227, 0.099609375).astype(jnp.bfloat16)
    energies = jnp.clip(-3.0 + 2.0 * jax.random.uniform(splits[2], (SAMPLES,), jnp.float32) ** levels(splits[2], (SAMPLES,), ((0, 8),), -0.2, 0.2), -3.0, -1.0)
    return dict(activations=activations, cotangents=cotangents, energies=energies)


reg_shift = 0.1

def block_grads(pair):
    acts, cots = pair
    sample_count = acts.shape[0]
    field = cots.astype(jnp.float32).reshape(sample_count, LAYERS, C, SIDE, SIDE)
    shifted = [jnp.roll(field, (row_step - 1, col_step - 1), axis=(3, 4)) for row_step in range(3) for col_step in range(3)]
    stacked = jnp.stack(shifted, axis=3).reshape(sample_count, LAYERS, C * 9, SIDE * SIDE)
    grads = jnp.einsum('slkx,slix->slki', stacked, acts.astype(jnp.float32), precision=lax.Precision.HIGHEST)
    grads = grads.reshape(sample_count, LAYERS, C, 9, C).transpose(0, 2, 1, 4, 3)
    return grads.reshape(sample_count, C * LAYERS * C * 9)

def reference(activations, cotangents, energies):
    total = activations.shape[0]
    params_all = LAYERS * C * C * 9
    acts = activations.reshape(N_SAMP, total // N_SAMP, LAYERS, C, SIDE * SIDE)
    cots = cotangents.reshape(N_SAMP, total // N_SAMP, LAYERS, C, SIDE * SIDE)
    grads = lax.map(block_grads, (acts, cots)).reshape(total, params_all)
    col_mean = lax.optimization_barrier(jnp.sum(grads, axis=0)) / total
    energy_mean = jnp.sum(energies) / total
    centered = ((grads - col_mean) * (1.0 / math.sqrt(params_all))).astype(jnp.bfloat16)
    deviation = energies - energy_mean
    gram = jnp.dot(centered.astype(jnp.float32), centered.T.astype(jnp.float32), preferred_element_type=jnp.float32)
    regular = gram + reg_shift * jnp.eye(total, dtype=jnp.float32)
    factor = jnp.linalg.cholesky(regular)
    forward = lax.linalg.triangular_solve(factor, deviation[:, None], left_side=True, lower=True)
    coeffs = lax.linalg.triangular_solve(factor, forward, left_side=True, lower=True, transpose_a=True)[:, 0]
    term = jnp.dot(coeffs[None, :], centered.astype(jnp.float32), precision=lax.Precision.HIGHEST)[0]
    update = -math.sqrt(params_all / total) * term
    return (update.reshape(C, LAYERS * C * 9), coeffs)
```

```python
import functools
import math

import jax
import jax.numpy as jnp
from jax import lax
from jax.experimental import pallas as pl
from jax.experimental.pallas import tpu as pltpu
from jax.sharding import PartitionSpec as P

C = 64
SIDE = 16
LAYERS = 2
SITES = SIDE * SIDE
OFFSETS = 9
LANES = 128
CORES = 2


reg_shift = 0.1
F32 = jnp.float32
BF16 = jnp.bfloat16
VMEM_LIMIT = 48 * 1024 * 1024


def kernel_call(body, out_shape, scratch_shapes=()):
    return pl.pallas_call(
        body,
        out_shape=out_shape,
        scratch_shapes=scratch_shapes,
        compiler_params=pltpu.CompilerParams(vmem_limit_bytes=VMEM_LIMIT),
    )


def swap(x, axis, mask):
    count = lax.axis_size(axis)
    return lax.ppermute(x, axis, [(i, i ^ mask) for i in range(count)])


def grads_body(acts_ref, cots_ref, keep_ref, send_ref, shifted_ref):
    samples, layers, owned, sites = cots_ref.shape
    half = owned // CORES
    core = lax.axis_index("samp") % CORES
    field = cots_ref[...].reshape(samples * layers, CORES, half, sites).astype(F32)
    swapped = jnp.concatenate([field[:, 1:], field[:, :1]], axis=1)
    field = jnp.where(core == 1, swapped, field).reshape(samples * layers * owned, sites).astype(BF16)
    source = lax.broadcasted_iota(jnp.int32, (sites, sites), 0)
    target = lax.broadcasted_iota(jnp.int32, (1, sites), 1)
    for offset in range(OFFSETS):
        row, col = target // SIDE, target % SIDE
        row = (row + SIDE - (offset // 3 - 1)) % SIDE
        col = (col + SIDE - (offset % 3 - 1)) % SIDE
        move = jnp.where(source == row * SIDE + col, 1.0, 0.0).astype(BF16)
        shifted_ref[offset] = jnp.dot(field, move, preferred_element_type=F32).astype(BF16)
    empty = jnp.zeros((C, sites), BF16)
    for sample in range(samples):
        left = []
        for layer in range(layers):
            first = (sample * layers + layer) * owned
            left.append(jnp.concatenate([shifted_ref[k, first : first + owned, :] for k in range(OFFSETS)], axis=0))
        right = [
            jnp.concatenate([acts_ref[sample, layer] if layer == other else empty for other in range(layers)], axis=1)
            for layer in range(layers)
        ]
        grads = lax.dot_general(
            jnp.concatenate(left, axis=1),
            jnp.concatenate(right, axis=0),
            (((1,), (1,)), ((), ())),
            preferred_element_type=F32,
        )
        for k in range(OFFSETS):
            rows = pl.ds(k * half * samples + sample, half, stride=samples)
            keep_ref[rows, :] = grads[k * owned : k * owned + half]
            send_ref[rows, :] = grads[k * owned + half : (k + 1) * owned]


def pack_body(keep_ref, recv_ref, *out_refs):
    offsets, chips, owned, samples, lanes = keep_ref.shape
    rows = offsets * owned
    position = lax.axis_index("samp")
    core, chip = position % CORES, position // CORES
    own_ref = out_refs[0]
    mine = pl.multiple_of(core * samples, samples)
    other = pl.multiple_of((1 - core) * samples, samples)
    own_ref[:, pl.ds(mine, samples), :] = keep_ref[:, chip].reshape(rows, samples, lanes)
    own_ref[:, pl.ds(other, samples), :] = recv_ref[:, chip].reshape(rows, samples, lanes)
    for slot in range(1, chips):
        values_ref, side_ref = out_refs[2 * slot - 1], out_refs[2 * slot]
        first = keep_ref[:, chip ^ slot].reshape(rows, samples, lanes)
        second = recv_ref[:, chip ^ slot].reshape(rows, samples, lanes)
        mean = (jnp.sum(first, axis=1) + jnp.sum(second, axis=1)) * (1.0 / (2 * samples))
        first, second = first - mean[:, None, :], second - mean[:, None, :]
        top = jnp.maximum(jnp.max(jnp.abs(first), axis=0), jnp.max(jnp.abs(second), axis=0))
        top = jnp.maximum(jnp.max(top, axis=0, keepdims=True), 1e-30)
        scale = 32768.0 / top
        values_ref[:, pl.ds(mine, samples), :] = first * scale
        values_ref[:, pl.ds(other, samples), :] = second * scale
        side_ref[0:rows, :] = mean
        side_ref[rows : rows + 1, :] = top * (1.0 / 32768.0)


def gram_body(total, params_all, energies_ref, own_ref, *refs):
    rows, group, lanes = own_ref.shape
    chips = total // group
    centered_ref, gram_ref = refs[2 * (chips - 1) :]
    chip = lax.axis_index("samp") // CORES
    gram = jnp.zeros((total, total), F32)
    pair = []
    for row in range(rows):
        blocks = [own_ref[row]]
        for slot in range(1, chips):
            values_ref, side_ref = refs[2 * slot - 2], refs[2 * slot - 1]
            blocks.append(values_ref[row] * side_ref[rows : rows + 1, :] + side_ref[row : row + 1, :])
        mean = sum(jnp.sum(block, axis=0, keepdims=True) for block in blocks) / total
        for slot in range(chips):
            place = pl.ds(pl.multiple_of((chip ^ slot) * group, group), group)
            centered_ref[row, place, :] = ((blocks[slot] - mean) * (1.0 / math.sqrt(params_all))).astype(BF16)
        pair.append(centered_ref[row])
        if len(pair) == 2 or row == rows - 1:
            both = jnp.concatenate(pair, axis=1)
            gram = gram + lax.dot_general(both, both, (((1,), (1,)), ((), ())), preferred_element_type=F32)
            pair = []
    gram_ref[0:total, :] = gram
    gram_ref[total : total + 8, :] = energies_ref[...]


def update_body(scale, coeffs_ref, centered_ref, update_ref):
    rows, total, lanes = centered_ref.shape
    coeffs = coeffs_ref[...] * scale
    terms = [jnp.sum(centered_ref[row].astype(F32) * coeffs, axis=0, keepdims=True) for row in range(rows)]
    owned = rows // OFFSETS
    padded = -(-rows // 8) * 8
    table = jnp.concatenate(terms + [jnp.zeros((padded - rows, lanes), F32)], axis=0)
    row_index = lax.broadcasted_iota(jnp.int32, (padded, lanes), 0)
    for tile in range(OFFSETS):
        place = lax.broadcasted_iota(jnp.int32, (padded, lanes), 1) + tile * lanes
        picked = jnp.take_along_axis(table, place // OFFSETS, axis=1)
        for channel in range(owned):
            mask = row_index == (place % OFFSETS) * owned + channel
            update_ref[channel : channel + 1, tile * lanes : (tile + 1) * lanes] = jnp.sum(
                jnp.where(mask, picked, 0.0), axis=0, keepdims=True
            )


def in_order(x, axis, mask):
    other = swap(x, axis, mask)
    low = (lax.axis_index(axis) & mask) == 0
    return jnp.where(low, jnp.concatenate([x, other]), jnp.concatenate([other, x]))


def solve_system(gram, dev_all, total):
    regular = gram + reg_shift * jnp.eye(total, dtype=F32)
    factor = jnp.linalg.cholesky(regular)
    forward = lax.linalg.triangular_solve(factor, dev_all[:, None], left_side=True, lower=True)
    return lax.linalg.triangular_solve(factor, forward, left_side=True, lower=True, transpose_a=True)[:, 0]


def local_split(activations, cotangents, energies):
    samples, layers, channels, sites = activations.shape
    owned = cotangents.shape[2]
    members = lax.axis_size("samp")
    chips = members // CORES
    group = CORES * samples
    total = members * samples
    position = lax.axis_index("samp")
    params_all = LAYERS * C * C * OFFSETS
    mine = owned // members
    rows = OFFSETS * mine

    half_rows = OFFSETS * (owned // CORES) * samples
    half_grads = jax.ShapeDtypeStruct((half_rows, LANES), F32)
    keep, send = kernel_call(
        grads_body, (half_grads, half_grads), [pltpu.VMEM((OFFSETS, samples * layers * owned, sites), BF16)]
    )(activations, cotangents)
    recv = swap(send, "samp", 1)
    split = (OFFSETS, chips, mine, samples, LANES)
    block = jax.ShapeDtypeStruct((rows, group, LANES), F32)
    side = jax.ShapeDtypeStruct((-(-(rows + 1) // 8) * 8, LANES), F32)
    packed = kernel_call(pack_body, (block,) + (block, side) * (chips - 1))(keep.reshape(split), recv.reshape(split))
    arrived = []
    for slot in range(1, chips):
        values, means = packed[2 * slot - 1], packed[2 * slot]
        arrived.append(swap(values.astype(jnp.float16), "samp", CORES * slot).astype(F32))
        arrived.append(swap(means, "samp", CORES * slot))

    lane = jnp.arange(total) // samples
    here = (lane == position) & (lax.axis_index("par") == 0)
    spread = jnp.where(here, jnp.tile(energies, members), 0.0)
    spread = jnp.where(jnp.arange(8)[:, None] == 0, spread[None, :], 0.0)
    centered, partial_gram = kernel_call(
        functools.partial(gram_body, total, params_all),
        (jax.ShapeDtypeStruct((rows, total, LANES), BF16), jax.ShapeDtypeStruct((total + 8, total), F32)),
    )(spread, packed[0], *arrived)

    summed = partial_gram + swap(partial_gram, "samp", 1)
    mask = 1
    while mask < lax.axis_size("par"):
        summed = summed + swap(summed, "par", mask)
        mask *= 2
    summed = summed + sum(swap(summed, "samp", CORES * slot) for slot in range(1, chips))

    energies_all = summed[total]
    deviation = energies_all - jnp.sum(energies_all) / total
    coeffs = solve_system(summed[:total], deviation, total)
    local_coeffs = lax.dynamic_slice_in_dim(coeffs, position * samples, samples)
    update = kernel_call(
        functools.partial(update_body, -math.sqrt(params_all / total)),
        jax.ShapeDtypeStruct((mine, OFFSETS * LANES), F32),
    )(coeffs[:, None], centered)
    mask = CORES
    while mask < members:
        update = in_order(update, "samp", mask)
        mask *= 2
    return in_order(update, "samp", 1), local_coeffs


def local_gather(activations, cotangents, energies):
    samples, layers, channels, sites = activations.shape
    owned = cotangents.shape[2]
    position = lax.axis_index("samp")
    total = lax.axis_size("samp") * samples
    params_all = LAYERS * C * C * OFFSETS
    field = cotangents.reshape(samples, layers, owned, SIDE, SIDE)
    shifted = [jnp.roll(field, (row - 1, col - 1), axis=(3, 4)) for row in range(3) for col in range(3)]
    stacked = jnp.stack(shifted, axis=3).reshape(samples, layers, owned * OFFSETS, sites)
    grads = jnp.einsum("slkx,slix->slki", stacked, activations, preferred_element_type=F32)
    grads = grads.reshape(samples, layers, owned, OFFSETS, channels).transpose(0, 2, 1, 4, 3)
    grads = grads.reshape(samples, owned * layers * channels * OFFSETS)
    col_sums, energy_sum = lax.psum((jnp.sum(grads, axis=0), jnp.sum(energies)), "samp")
    centered = ((grads - col_sums / total) * (1.0 / math.sqrt(params_all))).astype(BF16)
    everyone = lax.all_gather(centered, "samp", axis=0, tiled=True)
    partial_gram = lax.dot_general(centered, everyone, (((1,), (1,)), ((), ())), preferred_element_type=F32)
    gram = lax.all_gather(lax.psum(partial_gram, "par"), "samp", axis=0, tiled=True)
    deviation = lax.all_gather(energies - energy_sum / total, "samp", axis=0, tiled=True)
    coeffs = solve_system(gram, deviation, total)
    local_coeffs = lax.dynamic_slice_in_dim(coeffs, position * samples, samples)
    term = jnp.dot(local_coeffs[None, :], centered.astype(F32), precision=lax.Precision.HIGHEST)[0]
    update = -math.sqrt(params_all / total) * lax.psum(term, "samp")
    return update.reshape(owned, -1), local_coeffs


def local(activations, cotangents, energies):
    if cotangents.shape[2] % lax.axis_size("samp"):
        return local_gather(activations, cotangents, energies)
    return local_split(activations, cotangents, energies)


def solution(mesh):
    return jax.shard_map(
        local,
        mesh=mesh,
        in_specs=(P("samp", None, None, None), P("samp", None, "par", None), P("samp")),
        out_specs=(P("par", None), P("samp")),
        check_vma=False,
    )
```

```python
import functools
import math

import jax
import jax.numpy as jnp
from jax import lax
from jax.experimental import pallas as pl
from jax.experimental.pallas import tpu as pltpu
from jax.sharding import PartitionSpec as P

C = 64
SIDE = 16
LAYERS = 2
SITES = SIDE * SIDE
OFFSETS = 9
LANES = 128
CORES = 2


reg_shift = 0.1
F32 = jnp.float32
BF16 = jnp.bfloat16
VMEM_LIMIT = 48 * 1024 * 1024


def kernel_call(body, out_shape, scratch_shapes=()):
    return pl.pallas_call(
        body,
        out_shape=out_shape,
        scratch_shapes=scratch_shapes,
        compiler_params=pltpu.CompilerParams(vmem_limit_bytes=VMEM_LIMIT),
    )


def swap(x, axis, mask):
    count = lax.axis_size(axis)
    return lax.ppermute(x, axis, [(i, i ^ mask) for i in range(count)])


def grads_body(acts_ref, cots_ref, keep_ref, send_ref, shifted_ref):
    samples, layers, owned, sites = cots_ref.shape
    half = owned // CORES
    core = lax.axis_index("samp") % CORES
    field = cots_ref[...].reshape(samples * layers, CORES, half, sites).astype(F32)
    swapped = jnp.concatenate([field[:, 1:], field[:, :1]], axis=1)
    field = jnp.where(core == 1, swapped, field).reshape(samples * layers * owned, sites).astype(BF16)
    source = lax.broadcasted_iota(jnp.int32, (sites, sites), 0)
    target = lax.broadcasted_iota(jnp.int32, (1, sites), 1)
    for offset in range(OFFSETS):
        row, col = target // SIDE, target % SIDE
        row = (row + SIDE - (offset // 3 - 1)) % SIDE
        col = (col + SIDE - (offset % 3 - 1)) % SIDE
        move = jnp.where(source == row * SIDE + col, 1.0, 0.0).astype(BF16)
        shifted_ref[offset] = jnp.dot(field, move, preferred_element_type=F32).astype(BF16)
    empty = jnp.zeros((C, sites), BF16)
    for sample in range(samples):
        left = []
        for layer in range(layers):
            first = (sample * layers + layer) * owned
            left.append(jnp.concatenate([shifted_ref[k, first : first + owned, :] for k in range(OFFSETS)], axis=0))
        right = [
            jnp.concatenate([acts_ref[sample, layer] if layer == other else empty for other in range(layers)], axis=1)
            for layer in range(layers)
        ]
        grads = lax.dot_general(
            jnp.concatenate(left, axis=1),
            jnp.concatenate(right, axis=0),
            (((1,), (1,)), ((), ())),
            preferred_element_type=F32,
        )
        for k in range(OFFSETS):
            rows = pl.ds(k * half * samples + sample, half, stride=samples)
            keep_ref[rows, :] = grads[k * owned : k * owned + half]
            send_ref[rows, :] = grads[k * owned + half : (k + 1) * owned]


def pack_body(keep_ref, recv_ref, *out_refs):
    offsets, chips, owned, samples, lanes = keep_ref.shape
    rows = offsets * owned
    position = lax.axis_index("samp")
    core, chip = position % CORES, position // CORES
    own_ref = out_refs[0]
    mine = pl.multiple_of(core * samples, samples)
    other = pl.multiple_of((1 - core) * samples, samples)
    own_ref[:, pl.ds(mine, samples), :] = keep_ref[:, chip].reshape(rows, samples, lanes)
    own_ref[:, pl.ds(other, samples), :] = recv_ref[:, chip].reshape(rows, samples, lanes)
    for slot in range(1, chips):
        values_ref, side_ref = out_refs[2 * slot - 1], out_refs[2 * slot]
        first = keep_ref[:, chip ^ slot].reshape(rows, samples, lanes)
        second = recv_ref[:, chip ^ slot].reshape(rows, samples, lanes)
        mean = (jnp.sum(first, axis=1) + jnp.sum(second, axis=1)) * (1.0 / (2 * samples))
        first, second = first - mean[:, None, :], second - mean[:, None, :]
        top = jnp.maximum(jnp.max(jnp.abs(first), axis=0), jnp.max(jnp.abs(second), axis=0))
        top = jnp.maximum(jnp.max(top, axis=0, keepdims=True), 1e-30)
        scale = 32768.0 / top
        values_ref[:, pl.ds(mine, samples), :] = first * scale
        values_ref[:, pl.ds(other, samples), :] = second * scale
        side_ref[0:rows, :] = mean
        side_ref[rows : rows + 1, :] = top * (1.0 / 32768.0)


def gram_body(total, params_all, energies_ref, own_ref, *refs):
    rows, group, lanes = own_ref.shape
    chips = total // group
    centered_ref, gram_ref = refs[2 * (chips - 1) :]
    chip = lax.axis_index("samp") // CORES
    gram = jnp.zeros((total, total), F32)
    pair = []
    for row in range(rows):
        blocks = [own_ref[row]]
        for slot in range(1, chips):
            values_ref, side_ref = refs[2 * slot - 2], refs[2 * slot - 1]
            blocks.append(values_ref[row] * side_ref[rows : rows + 1, :] + side_ref[row : row + 1, :])
        mean = sum(jnp.sum(block, axis=0, keepdims=True) for block in blocks) / total
        for slot in range(chips):
            place = pl.ds(pl.multiple_of((chip ^ slot) * group, group), group)
            centered_ref[row, place, :] = ((blocks[slot] - mean) * (1.0 / math.sqrt(params_all))).astype(BF16)
        pair.append(centered_ref[row])
        if len(pair) == 2 or row == rows - 1:
            both = jnp.concatenate(pair, axis=1)
            gram = gram + lax.dot_general(both, both, (((1,), (1,)), ((), ())), preferred_element_type=F32)
            pair = []
    gram_ref[0:total, :] = gram
    gram_ref[total : total + 8, :] = energies_ref[...]


def invert(matrix):
    size = 8 * len(matrix)
    row = lax.broadcasted_iota(jnp.int32, (8, size), 0)
    lane = lax.broadcasted_iota(jnp.int32, (8, size), 1)
    matrix = list(matrix)
    for pivot in range(len(matrix)):
        first = 8 * pivot
        spread = [[jnp.broadcast_to(rows[:, first + c : first + c + 1], (8, size)) for c in range(8)] for rows in matrix]
        inside = (lane >= first) & (lane < first + 8)
        panel = jnp.where(inside, jnp.where(lane == row + first, 1.0, 0.0), matrix[pivot])
        block = spread[pivot]
        for step in range(8):
            inverse = 1.0 / block[step][step : step + 1]
            column, here = block[step], row == step
            scaled = panel[step : step + 1] * inverse
            panel = jnp.where(here, scaled, panel - column * scaled)
            for c in range(step + 1, 8):
                scaled = block[c][step : step + 1] * inverse
                block[c] = jnp.where(here, scaled, block[c] - column * scaled)
        for other in range(len(matrix)):
            if other != pivot:
                rows = jnp.where(inside, 0.0, matrix[other])
                for c in range(8):
                    rows = rows - spread[other][c] * panel[c : c + 1]
                matrix[other] = rows
        matrix[pivot] = panel
    return matrix


def solve_body(scale, centered_ref, *refs):
    *part_refs, update_ref, coeffs_ref = refs
    rows, total, lanes = centered_ref.shape
    samples = coeffs_ref.shape[1]
    summed = part_refs[0][...]
    for ref in part_refs[1:]:
        summed = summed + ref[...]
    row_index = lax.broadcasted_iota(jnp.int32, (8, total), 0)
    lane_index = lax.broadcasted_iota(jnp.int32, (8, total), 1)
    regular = [
        summed[first : first + 8] + jnp.where(lane_index == row_index + first, reg_shift, 0.0) for first in range(0, total, 8)
    ]
    energies = summed[total : total + 1]
    deviation = energies - jnp.sum(energies, axis=1, keepdims=True) / total
    coeffs = jnp.concatenate([jnp.sum(part * deviation, axis=1, keepdims=True) for part in invert(regular)], axis=0)

    position = lax.axis_index("samp")
    sample = lax.broadcasted_iota(jnp.int32, (total, lanes), 0)
    lane = lax.broadcasted_iota(jnp.int32, (total, lanes), 1)
    spread = jnp.broadcast_to(coeffs, (total, lanes))
    own = jnp.sum(jnp.where(sample == lane + position * samples, spread, 0.0), axis=0, keepdims=True)
    coeffs_ref[...] = own[:, :samples]

    spread = spread * scale
    terms = [jnp.sum(centered_ref[row].astype(F32) * spread, axis=0, keepdims=True) for row in range(rows)]
    owned = rows // OFFSETS
    padded = -(-rows // 8) * 8
    table = jnp.concatenate(terms + [jnp.zeros((padded - rows, lanes), F32)], axis=0)
    row_index = lax.broadcasted_iota(jnp.int32, (padded, lanes), 0)
    for tile in range(OFFSETS):
        place = lax.broadcasted_iota(jnp.int32, (padded, lanes), 1) + tile * lanes
        picked = jnp.take_along_axis(table, place // OFFSETS, axis=1)
        for channel in range(owned):
            mask = row_index == (place % OFFSETS) * owned + channel
            update_ref[channel : channel + 1, tile * lanes : (tile + 1) * lanes] = jnp.sum(
                jnp.where(mask, picked, 0.0), axis=0, keepdims=True
            )


def in_order(x, axis, mask):
    other = swap(x, axis, mask)
    low = (lax.axis_index(axis) & mask) == 0
    return jnp.where(low, jnp.concatenate([x, other]), jnp.concatenate([other, x]))


def solve_system(gram, dev_all, total):
    regular = gram + reg_shift * jnp.eye(total, dtype=F32)
    factor = jnp.linalg.cholesky(regular)
    forward = lax.linalg.triangular_solve(factor, dev_all[:, None], left_side=True, lower=True)
    return lax.linalg.triangular_solve(factor, forward, left_side=True, lower=True, transpose_a=True)[:, 0]


def local_split(activations, cotangents, energies):
    samples, layers, channels, sites = activations.shape
    owned = cotangents.shape[2]
    members = lax.axis_size("samp")
    chips = members // CORES
    group = CORES * samples
    total = members * samples
    position = lax.axis_index("samp")
    params_all = LAYERS * C * C * OFFSETS
    mine = owned // members
    rows = OFFSETS * mine

    half_rows = OFFSETS * (owned // CORES) * samples
    half_grads = jax.ShapeDtypeStruct((half_rows, LANES), F32)
    keep, send = kernel_call(
        grads_body, (half_grads, half_grads), [pltpu.VMEM((OFFSETS, samples * layers * owned, sites), BF16)]
    )(activations, cotangents)
    recv = swap(send, "samp", 1)
    split = (OFFSETS, chips, mine, samples, LANES)
    block = jax.ShapeDtypeStruct((rows, group, LANES), F32)
    side = jax.ShapeDtypeStruct((-(-(rows + 1) // 8) * 8, LANES), F32)
    packed = kernel_call(pack_body, (block,) + (block, side) * (chips - 1))(keep.reshape(split), recv.reshape(split))
    arrived = []
    for slot in range(1, chips):
        values, means = packed[2 * slot - 1], packed[2 * slot]
        arrived.append(swap(values.astype(jnp.float16), "samp", CORES * slot).astype(F32))
        arrived.append(swap(means, "samp", CORES * slot))

    lane = jnp.arange(total) // samples
    here = (lane == position) & (lax.axis_index("par") == 0)
    spread = jnp.where(here, jnp.tile(energies, members), 0.0)
    spread = jnp.where(jnp.arange(8)[:, None] == 0, spread[None, :], 0.0)
    centered, partial_gram = kernel_call(
        functools.partial(gram_body, total, params_all),
        (jax.ShapeDtypeStruct((rows, total, LANES), BF16), jax.ShapeDtypeStruct((total + 8, total), F32)),
    )(spread, packed[0], *arrived)

    summed = partial_gram + swap(partial_gram, "samp", 1)
    mask = 1
    while mask < lax.axis_size("par"):
        summed = summed + swap(summed, "par", mask)
        mask *= 2
    parts = [summed] + [swap(summed, "samp", CORES * slot) for slot in range(1, chips)]
    update, local_coeffs = kernel_call(
        functools.partial(solve_body, -math.sqrt(params_all / total)),
        (jax.ShapeDtypeStruct((mine, OFFSETS * LANES), F32), jax.ShapeDtypeStruct((1, samples), F32)),
    )(centered, *parts)
    mask = CORES
    while mask < members:
        update = in_order(update, "samp", mask)
        mask *= 2
    return in_order(update, "samp", 1), local_coeffs[0]


def local_gather(activations, cotangents, energies):
    samples, layers, channels, sites = activations.shape
    owned = cotangents.shape[2]
    position = lax.axis_index("samp")
    total = lax.axis_size("samp") * samples
    params_all = LAYERS * C * C * OFFSETS
    field = cotangents.reshape(samples, layers, owned, SIDE, SIDE)
    shifted = [jnp.roll(field, (row - 1, col - 1), axis=(3, 4)) for row in range(3) for col in range(3)]
    stacked = jnp.stack(shifted, axis=3).reshape(samples, layers, owned * OFFSETS, sites)
    grads = jnp.einsum("slkx,slix->slki", stacked, activations, preferred_element_type=F32)
    grads = grads.reshape(samples, layers, owned, OFFSETS, channels).transpose(0, 2, 1, 4, 3)
    grads = grads.reshape(samples, owned * layers * channels * OFFSETS)
    col_sums, energy_sum = lax.psum((jnp.sum(grads, axis=0), jnp.sum(energies)), "samp")
    centered = ((grads - col_sums / total) * (1.0 / math.sqrt(params_all))).astype(BF16)
    everyone = lax.all_gather(centered, "samp", axis=0, tiled=True)
    partial_gram = lax.dot_general(centered, everyone, (((1,), (1,)), ((), ())), preferred_element_type=F32)
    gram = lax.all_gather(lax.psum(partial_gram, "par"), "samp", axis=0, tiled=True)
    deviation = lax.all_gather(energies - energy_sum / total, "samp", axis=0, tiled=True)
    coeffs = solve_system(gram, deviation, total)
    local_coeffs = lax.dynamic_slice_in_dim(coeffs, position * samples, samples)
    term = jnp.dot(local_coeffs[None, :], centered.astype(F32), precision=lax.Precision.HIGHEST)[0]
    update = -math.sqrt(params_all / total) * lax.psum(term, "samp")
    return update.reshape(owned, -1), local_coeffs


def local(activations, cotangents, energies):
    if cotangents.shape[2] % lax.axis_size("samp"):
        return local_gather(activations, cotangents, energies)
    return local_split(activations, cotangents, energies)


def solution(mesh):
    return jax.shard_map(
        local,
        mesh=mesh,
        in_specs=(P("samp", None, None, None), P("samp", None, "par", None), P("samp")),
        out_specs=(P("par", None), P("samp")),
        check_vma=False,
    )
```

```python
import functools
import math

import jax
import jax.numpy as jnp
from jax import lax
from jax.experimental import pallas as pl
from jax.experimental.pallas import tpu as pltpu
from jax.sharding import PartitionSpec as P

C = 64
SIDE = 16
LAYERS = 2
SITES = SIDE * SIDE
OFFSETS = 9
LANES = 128
CORES = 2


reg_shift = 0.1
F32 = jnp.float32
BF16 = jnp.bfloat16
VMEM_LIMIT = 48 * 1024 * 1024


def kernel_call(body, out_shape, scratch_shapes=()):
    return pl.pallas_call(
        body,
        out_shape=out_shape,
        scratch_shapes=scratch_shapes,
        compiler_params=pltpu.CompilerParams(vmem_limit_bytes=VMEM_LIMIT),
    )


def swap(x, axis, mask):
    count = lax.axis_size(axis)
    return lax.ppermute(x, axis, [(i, i ^ mask) for i in range(count)])


def exponent(values):
    top = jnp.maximum(jnp.max(jnp.abs(values), axis=0, keepdims=True), 1e-30)
    return 14.0 - jnp.floor(jnp.log2(top))


def packed_rows(rows, samples):
    return -(-(rows * samples + rows + 2) // 8) * 8


def grads_body(acts_ref, cots_ref, own_ref, *refs):
    samples, layers, owned, sites = cots_ref.shape
    *out_refs, shifted_ref, grads_ref = refs
    members = len(out_refs) + 1
    mine = owned // members
    rows = OFFSETS * mine
    field = cots_ref[...].reshape(samples * layers * owned, sites)
    source = lax.broadcasted_iota(jnp.int32, (sites, sites), 0)
    target = lax.broadcasted_iota(jnp.int32, (1, sites), 1)
    for offset in range(OFFSETS):
        row, col = target // SIDE, target % SIDE
        row = (row + SIDE - (offset // 3 - 1)) % SIDE
        col = (col + SIDE - (offset % 3 - 1)) % SIDE
        move = jnp.where(source == row * SIDE + col, 1.0, 0.0).astype(BF16)
        shifted_ref[offset] = jnp.dot(field, move, preferred_element_type=F32).astype(BF16)
    empty = jnp.zeros((C, sites), BF16)
    for sample in range(samples):
        left = []
        for layer in range(layers):
            first = (sample * layers + layer) * owned
            left.append(jnp.concatenate([shifted_ref[k, first : first + owned, :] for k in range(OFFSETS)], axis=0))
        right = [
            jnp.concatenate([acts_ref[sample, layer] if layer == other else empty for other in range(layers)], axis=1)
            for layer in range(layers)
        ]
        grads_ref[pl.ds(sample, OFFSETS * owned, stride=samples), :] = lax.dot_general(
            jnp.concatenate(left, axis=1),
            jnp.concatenate(right, axis=0),
            (((1,), (1,)), ((), ())),
            preferred_element_type=F32,
        )
    position = lax.axis_index("samp")
    lanes = grads_ref.shape[1]
    for slot in range(members):
        start = (position ^ slot) * (mine * samples)
        pieces = [
            grads_ref[pl.ds(pl.multiple_of(k * owned * samples + start, mine * samples), mine * samples), :] for k in range(OFFSETS)
        ]
        values = jnp.concatenate(pieces, axis=0).reshape(rows, samples, lanes)
        if slot == 0:
            own_ref[...] = values
            continue
        values_ref = out_refs[slot - 1]
        reference = (jnp.sum(values, axis=1) * (1.0 / samples)).astype(BF16).astype(F32)
        values = values - reference[:, None, :]
        shift = exponent(jnp.max(jnp.abs(values), axis=0))
        reference_shift = exponent(reference)
        last = rows * samples
        values_ref[0:last, :] = (values * jnp.exp2(shift)).reshape(last, lanes)
        values_ref[last : last + rows, :] = reference * jnp.exp2(reference_shift)
        values_ref[last + rows : last + rows + 1, :] = shift
        values_ref[last + rows + 1 : last + rows + 2, :] = reference_shift
        spare = values_ref.shape[0] - (last + rows + 2)
        if spare:
            values_ref[last + rows + 2 :, :] = jnp.zeros((spare, lanes), F32)


def halves(half):
    row = lax.broadcasted_iota(jnp.int32, (half, 2 * half), 0)
    lane = lax.broadcasted_iota(jnp.int32, (half, 2 * half), 1)
    return row, lane


def fold(matrix, energies):
    half = matrix.shape[0] // 2
    row, lane = halves(half)
    top, bottom = matrix[:half], matrix[half:]
    turned = pltpu.roll(bottom, half, 1)
    diagonal = jnp.sum(jnp.where(lane == row, turned, 0.0), axis=0, keepdims=True)
    first = lax.broadcasted_iota(jnp.int32, energies.shape, 0) == 0
    rest = jnp.where(first, diagonal, energies)
    return jnp.concatenate([jnp.where((lane > row) & (lane < half), turned, top), rest], axis=0)


def unfold(folded):
    half = folded.shape[1] // 2
    row, lane = halves(half)
    body, diagonal = folded[:half], folded[half : half + 1]
    flipped = body.T
    mixed, crossed = flipped[:half], flipped[half:]
    both = jnp.concatenate([mixed, crossed], axis=1)
    top = jnp.where((lane > row) & (lane < half), both, body)
    lower = jnp.concatenate([crossed, mixed], axis=1)
    turned = pltpu.roll(body, half, 1)
    place = lane - half
    corner = jnp.where(place > row, turned, jnp.where(place == row, pltpu.roll(jnp.broadcast_to(diagonal, turned.shape), half, 1), lower))
    return jnp.concatenate([top, jnp.where(lane < half, lower, corner)], axis=0)


def gram_body(total, params_all, energies_ref, own_ref, *refs):
    rows, group, lanes = own_ref.shape
    *value_refs, centered_ref, gram_ref = refs
    by_slot = dict(zip(far_first(len(value_refs) + 1), value_refs))
    value_refs = [by_slot[slot] for slot in sorted(by_slot)]
    position = lax.axis_index("samp")
    gram = jnp.zeros((total, total), F32)
    last = rows * group
    scales = [jnp.exp2(-ref[last + rows : last + rows + 1, :]) for ref in value_refs]
    references = [ref[last : last + rows, :] * jnp.exp2(-ref[last + rows + 1 : last + rows + 2, :]) for ref in value_refs]
    pair = []
    for row in range(rows):
        blocks = [own_ref[row]]
        for ref, scale, reference in zip(value_refs, scales, references):
            blocks.append(ref[row * group : (row + 1) * group, :] * scale + reference[row : row + 1, :])
        mean = sum(jnp.sum(block, axis=0, keepdims=True) for block in blocks) / total
        for slot in range(len(blocks)):
            place = pl.ds(pl.multiple_of((position ^ slot) * group, group), group)
            centered_ref[row, place, :] = ((blocks[slot] - mean) * (1.0 / math.sqrt(params_all))).astype(BF16)
        pair.append(centered_ref[row])
        if len(pair) == 2 or row == rows - 1:
            both = jnp.concatenate(pair, axis=1)
            gram = gram + lax.dot_general(both, both, (((1,), (1,)), ((), ())), preferred_element_type=F32)
            pair = []
    gram_ref[...] = fold(gram, energies_ref[...])


def invert(matrix):
    size = 8 * len(matrix)
    row = lax.broadcasted_iota(jnp.int32, (8, size), 0)
    lane = lax.broadcasted_iota(jnp.int32, (8, size), 1)
    matrix = list(matrix)
    for pivot in range(len(matrix)):
        first = 8 * pivot
        spread = [[jnp.broadcast_to(rows[:, first + c : first + c + 1], (8, size)) for c in range(8)] for rows in matrix]
        inside = (lane >= first) & (lane < first + 8)
        panel = jnp.where(inside, jnp.where(lane == row + first, 1.0, 0.0), matrix[pivot])
        block = spread[pivot]
        for step in range(8):
            inverse = 1.0 / block[step][step : step + 1]
            column, here = block[step], row == step
            scaled = panel[step : step + 1] * inverse
            panel = jnp.where(here, scaled, panel - column * scaled)
            for c in range(step + 1, 8):
                scaled = block[c][step : step + 1] * inverse
                block[c] = jnp.where(here, scaled, block[c] - column * scaled)
        for other in range(len(matrix)):
            if other != pivot:
                rows = jnp.where(inside, 0.0, matrix[other])
                for c in range(8):
                    rows = rows - spread[other][c] * panel[c : c + 1]
                matrix[other] = rows
        matrix[pivot] = panel
    return matrix


def solve_body(scale, centered_ref, *refs):
    *part_refs, update_ref, coeffs_ref = refs
    rows, total, lanes = centered_ref.shape
    samples = coeffs_ref.shape[1]
    summed = part_refs[0][...]
    for ref in part_refs[1:]:
        summed = summed + ref[...]
    matrix = unfold(summed)
    row_index = lax.broadcasted_iota(jnp.int32, (8, total), 0)
    lane_index = lax.broadcasted_iota(jnp.int32, (8, total), 1)
    regular = [
        matrix[first : first + 8] + jnp.where(lane_index == row_index + first, reg_shift, 0.0) for first in range(0, total, 8)
    ]
    energies = summed[total // 2 + 1 : total // 2 + 2]
    deviation = energies - jnp.sum(energies, axis=1, keepdims=True) / total
    coeffs = jnp.concatenate([jnp.sum(part * deviation, axis=1, keepdims=True) for part in invert(regular)], axis=0)

    position = lax.axis_index("samp")
    sample = lax.broadcasted_iota(jnp.int32, (total, lanes), 0)
    lane = lax.broadcasted_iota(jnp.int32, (total, lanes), 1)
    spread = jnp.broadcast_to(coeffs, (total, lanes))
    own = jnp.sum(jnp.where(sample == lane + position * samples, spread, 0.0), axis=0, keepdims=True)
    coeffs_ref[...] = own[:, :samples]

    spread = spread * scale
    terms = [jnp.sum(centered_ref[row].astype(F32) * spread, axis=0, keepdims=True) for row in range(rows)]
    owned = rows // OFFSETS
    padded = -(-rows // 8) * 8
    table = jnp.concatenate(terms + [jnp.zeros((padded - rows, lanes), F32)], axis=0)
    row_index = lax.broadcasted_iota(jnp.int32, (padded, lanes), 0)
    for tile in range(OFFSETS):
        place = lax.broadcasted_iota(jnp.int32, (padded, lanes), 1) + tile * lanes
        picked = jnp.take_along_axis(table, place // OFFSETS, axis=1)
        for channel in range(owned):
            mask = row_index == (place % OFFSETS) * owned + channel
            update_ref[channel : channel + 1, tile * lanes : (tile + 1) * lanes] = jnp.sum(
                jnp.where(mask, picked, 0.0), axis=0, keepdims=True
            )


def far_first(members):
    far = range(2 * CORES, members)
    return [CORES, *far, *range(CORES + 1, 2 * CORES), *range(1, CORES)]


def swaps(x, axis, masks):
    return {mask: swap(x, axis, mask) for mask in sorted(masks, reverse=True)}


def in_order(x, axis, masks):
    blocks = {0: x, **swaps(x, axis, masks)}
    bits = lax.axis_index(axis) & functools.reduce(lambda a, b: a | b, masks)
    placed = []
    for place in sorted(blocks):
        block = blocks[0]
        for mask in sorted(masks):
            block = jnp.where(bits == place ^ mask, blocks[mask], block)
        placed.append(block)
    return jnp.concatenate(placed)


def solve_system(gram, dev_all, total):
    regular = gram + reg_shift * jnp.eye(total, dtype=F32)
    factor = jnp.linalg.cholesky(regular)
    forward = lax.linalg.triangular_solve(factor, dev_all[:, None], left_side=True, lower=True)
    return lax.linalg.triangular_solve(factor, forward, left_side=True, lower=True, transpose_a=True)[:, 0]


def local_split(activations, cotangents, energies):
    samples, layers, channels, sites = activations.shape
    owned = cotangents.shape[2]
    members = lax.axis_size("samp")
    chips = members // CORES
    total = members * samples
    position = lax.axis_index("samp")
    params_all = LAYERS * C * C * OFFSETS
    mine = owned // members
    rows = OFFSETS * mine

    own = jax.ShapeDtypeStruct((rows, samples, LANES), F32)
    block = jax.ShapeDtypeStruct((packed_rows(rows, samples), LANES), F32)
    own, *blocks = kernel_call(
        grads_body,
        (own,) + (block,) * (members - 1),
        [
            pltpu.VMEM((OFFSETS, samples * layers * owned, sites), BF16),
            pltpu.VMEM((OFFSETS * owned * samples, LANES), F32),
        ],
    )(activations, cotangents)
    order = far_first(members)
    arrived = [swap(blocks[slot - 1].astype(jnp.float16), "samp", slot).astype(F32) for slot in order]

    lane = jnp.arange(total) // samples
    here = (lane == position) & (lax.axis_index("par") == 0)
    spread = jnp.where(here, jnp.tile(energies, members), 0.0)
    spread = jnp.where(jnp.arange(8)[:, None] == 1, spread[None, :], 0.0)
    centered, partial_gram = kernel_call(
        functools.partial(gram_body, total, params_all),
        (jax.ShapeDtypeStruct((rows, total, LANES), BF16), jax.ShapeDtypeStruct((total // 2 + 8, total), F32)),
    )(spread, own, *arrived)

    summed = partial_gram + swap(partial_gram, "samp", 1)
    summed = summed + sum(swaps(summed, "par", range(1, lax.axis_size("par"))).values())
    parts = [summed, *swaps(summed, "samp", range(CORES, members, CORES)).values()]
    update, local_coeffs = kernel_call(
        functools.partial(solve_body, -math.sqrt(params_all / total)),
        (jax.ShapeDtypeStruct((mine, OFFSETS * LANES), F32), jax.ShapeDtypeStruct((1, samples), F32)),
    )(centered, *parts)
    update = in_order(update, "samp", range(1, CORES))
    update = in_order(update, "samp", range(CORES, members, CORES))
    return update, local_coeffs[0]


def local_gather(activations, cotangents, energies):
    samples, layers, channels, sites = activations.shape
    owned = cotangents.shape[2]
    position = lax.axis_index("samp")
    total = lax.axis_size("samp") * samples
    params_all = LAYERS * C * C * OFFSETS
    field = cotangents.reshape(samples, layers, owned, SIDE, SIDE)
    shifted = [jnp.roll(field, (row - 1, col - 1), axis=(3, 4)) for row in range(3) for col in range(3)]
    stacked = jnp.stack(shifted, axis=3).reshape(samples, layers, owned * OFFSETS, sites)
    grads = jnp.einsum("slkx,slix->slki", stacked, activations, preferred_element_type=F32)
    grads = grads.reshape(samples, layers, owned, OFFSETS, channels).transpose(0, 2, 1, 4, 3)
    grads = grads.reshape(samples, owned * layers * channels * OFFSETS)
    col_sums, energy_sum = lax.psum((jnp.sum(grads, axis=0), jnp.sum(energies)), "samp")
    centered = ((grads - col_sums / total) * (1.0 / math.sqrt(params_all))).astype(BF16)
    everyone = lax.all_gather(centered, "samp", axis=0, tiled=True)
    partial_gram = lax.dot_general(centered, everyone, (((1,), (1,)), ((), ())), preferred_element_type=F32)
    gram = lax.all_gather(lax.psum(partial_gram, "par"), "samp", axis=0, tiled=True)
    deviation = lax.all_gather(energies - energy_sum / total, "samp", axis=0, tiled=True)
    coeffs = solve_system(gram, deviation, total)
    local_coeffs = lax.dynamic_slice_in_dim(coeffs, position * samples, samples)
    term = jnp.dot(local_coeffs[None, :], centered.astype(F32), precision=lax.Precision.HIGHEST)[0]
    update = -math.sqrt(params_all / total) * lax.psum(term, "samp")
    return update.reshape(owned, -1), local_coeffs


def local(activations, cotangents, energies):
    if cotangents.shape[2] % lax.axis_size("samp"):
        return local_gather(activations, cotangents, energies)
    return local_split(activations, cotangents, energies)


def solution(mesh):
    return jax.shard_map(
        local,
        mesh=mesh,
        in_specs=(P("samp", None, None, None), P("samp", None, "par", None), P("samp")),
        out_specs=(P("par", None), P("samp")),
        check_vma=False,
    )
```

```python
import functools
import math

import jax
import jax.numpy as jnp
from jax import lax
from jax.experimental import pallas as pl
from jax.experimental.pallas import tpu as pltpu
from jax.sharding import PartitionSpec as P

C = 64
SIDE = 16
LAYERS = 2
SITES = SIDE * SIDE
OFFSETS = 9
LANES = 128
CORES = 2


reg_shift = 0.1
F32 = jnp.float32
BF16 = jnp.bfloat16
VMEM_LIMIT = 48 * 1024 * 1024


def kernel_call(body, out_shape, scratch_shapes=(), **options):
    return pl.pallas_call(
        body,
        out_shape=out_shape,
        **options,
        scratch_shapes=scratch_shapes,
        compiler_params=pltpu.CompilerParams(vmem_limit_bytes=VMEM_LIMIT),
    )


def swap(x, axis, mask):
    count = lax.axis_size(axis)
    return lax.ppermute(x, axis, [(i, i ^ mask) for i in range(count)])


def exponent(values):
    top = jnp.maximum(jnp.max(jnp.abs(values), axis=0, keepdims=True), 1e-30)
    return 14.0 - jnp.floor(jnp.log2(top))


def packed_rows(rows, samples):
    return -(-(rows * samples + rows + 2) // 8) * 8


def grads_body(far, acts_hbm, cots_hbm, *refs):
    *out_refs, acts_ref, cots_ref, shifted_ref, grads_ref, semaphores = refs
    copies = [
        pltpu.make_async_copy(cots_hbm, cots_ref, semaphores.at[0]),
        pltpu.make_async_copy(acts_hbm, acts_ref, semaphores.at[1]),
    ]
    for copy in copies:
        copy.start()
    samples, layers, owned, sites = cots_ref.shape
    members = len(out_refs)
    owned = owned // 2
    mine = owned // members
    rows = OFFSETS * mine
    moves = []
    source = lax.broadcasted_iota(jnp.int32, (sites, sites), 0)
    target = lax.broadcasted_iota(jnp.int32, (1, sites), 1)
    for offset in range(OFFSETS):
        row, col = target // SIDE, target % SIDE
        row = (row + SIDE - (offset // 3 - 1)) % SIDE
        col = (col + SIDE - (offset % 3 - 1)) % SIDE
        moves.append(jnp.where(source == row * SIDE + col, 1.0, 0.0).astype(BF16))
    position = lax.axis_index("samp")
    upper = (position // members + int(far)) % 2 == 1
    copies[0].wait()
    field = cots_ref[...].astype(F32).reshape(samples * layers, 2, owned, sites)
    field = jnp.where(upper, field[:, 1], field[:, 0]).reshape(samples * layers * owned, sites).astype(BF16)
    for offset in range(OFFSETS):
        shifted_ref[offset] = jnp.dot(field, moves[offset], preferred_element_type=F32).astype(BF16)
    copies[1].wait()
    lanes = grads_ref.shape[1]
    lane = lax.broadcasted_iota(jnp.int32, (OFFSETS, owned, lanes), 2)
    for sample in range(samples):
        first = sample * layers * owned
        left = jnp.concatenate([shifted_ref[k, first : first + layers * owned, :] for k in range(OFFSETS)], axis=0)
        right = acts_ref[sample].reshape(layers * C, sites)
        products = lax.dot_general(left, right, (((1,), (1,)), ((), ())), preferred_element_type=F32)
        products = products.reshape(OFFSETS, layers, owned, lanes)
        grads = products[:, 0]
        for layer in range(1, layers):
            grads = jnp.where(lane >= layer * C, products[:, layer], grads)
        grads_ref[pl.ds(sample, OFFSETS * owned, stride=samples), :] = grads.reshape(OFFSETS * owned, lanes)
    for index in range(members):
        slot = index + members * int(far)
        start = ((position ^ slot) % members) * (mine * samples)
        pieces = [
            grads_ref[pl.ds(pl.multiple_of(k * owned * samples + start, mine * samples), mine * samples), :] for k in range(OFFSETS)
        ]
        values = jnp.concatenate(pieces, axis=0).reshape(rows, samples, lanes)
        values_ref = out_refs[index]
        if slot == 0:
            values_ref[...] = values
            continue
        reference = (jnp.sum(values, axis=1) * (1.0 / samples)).astype(BF16).astype(F32)
        values = values - reference[:, None, :]
        shift = exponent(jnp.max(jnp.abs(values), axis=0))
        reference_shift = exponent(reference)
        last = rows * samples
        values_ref[0:last, :] = (values * jnp.exp2(shift)).reshape(last, lanes)
        values_ref[last : last + rows, :] = reference * jnp.exp2(reference_shift)
        values_ref[last + rows : last + rows + 1, :] = shift
        values_ref[last + rows + 1 : last + rows + 2, :] = reference_shift
        spare = values_ref.shape[0] - (last + rows + 2)
        if spare:
            values_ref[last + rows + 2 :, :] = jnp.zeros((spare, lanes), F32)


def halves(half):
    row = lax.broadcasted_iota(jnp.int32, (half, 2 * half), 0)
    lane = lax.broadcasted_iota(jnp.int32, (half, 2 * half), 1)
    return row, lane


def fold(matrix, energies):
    half = matrix.shape[0] // 2
    row, lane = halves(half)
    top, bottom = matrix[:half], matrix[half:]
    turned = pltpu.roll(bottom, half, 1)
    diagonal = jnp.sum(jnp.where(lane == row, turned, 0.0), axis=0, keepdims=True)
    first = lax.broadcasted_iota(jnp.int32, energies.shape, 0) == 0
    rest = jnp.where(first, diagonal, energies)
    return jnp.concatenate([jnp.where((lane > row) & (lane < half), turned, top), rest], axis=0)


def unfold(folded):
    half = folded.shape[1] // 2
    row, lane = halves(half)
    body, diagonal = folded[:half], folded[half : half + 1]
    flipped = body.T
    mixed, crossed = flipped[:half], flipped[half:]
    both = jnp.concatenate([mixed, crossed], axis=1)
    top = jnp.where((lane > row) & (lane < half), both, body)
    lower = jnp.concatenate([crossed, mixed], axis=1)
    turned = pltpu.roll(body, half, 1)
    place = lane - half
    corner = jnp.where(place > row, turned, jnp.where(place == row, pltpu.roll(jnp.broadcast_to(diagonal, turned.shape), half, 1), lower))
    return jnp.concatenate([top, jnp.where(lane < half, lower, corner)], axis=0)


def gram_body(total, params_all, energies_ref, own_ref, *refs):
    rows, group, lanes = own_ref.shape
    *value_refs, centered_ref, gram_ref = refs
    by_slot = dict(zip(far_first(len(value_refs) + 1), value_refs))
    value_refs = [by_slot[slot] for slot in sorted(by_slot)]
    position = lax.axis_index("samp")
    gram = jnp.zeros((total, total), F32)
    last = rows * group
    scales = [jnp.exp2(-ref[last + rows : last + rows + 1, :]) for ref in value_refs]
    references = [ref[last : last + rows, :] * jnp.exp2(-ref[last + rows + 1 : last + rows + 2, :]) for ref in value_refs]
    pair = []
    for row in range(rows):
        blocks = [own_ref[row]]
        for ref, scale, reference in zip(value_refs, scales, references):
            blocks.append(ref[row * group : (row + 1) * group, :] * scale + reference[row : row + 1, :])
        mean = sum(jnp.sum(block, axis=0, keepdims=True) for block in blocks) / total
        for slot in range(len(blocks)):
            place = pl.ds(pl.multiple_of((position ^ slot) * group, group), group)
            centered_ref[row, place, :] = ((blocks[slot] - mean) * (1.0 / math.sqrt(params_all))).astype(BF16)
        pair.append(centered_ref[row])
        if len(pair) == 2 or row == rows - 1:
            both = jnp.concatenate(pair, axis=1)
            gram = gram + lax.dot_general(both, both, (((1,), (1,)), ((), ())), preferred_element_type=F32)
            pair = []
    gram_ref[...] = fold(gram, energies_ref[...])


def thirds(values):
    high = values.astype(BF16).astype(F32)
    middle = (values - high).astype(BF16).astype(F32)
    return high, middle, values - high - middle


def outer_sum(left, right):
    a, b, c = thirds(left)
    d, e, f = thirds(right)
    lefts = jnp.concatenate([a, a, b, a, b, c], axis=0).astype(BF16)
    rights = jnp.concatenate([d, e, d, f, e, d], axis=0).astype(BF16)
    return lax.dot_general(lefts, rights, (((0,), (0,)), ((), ())), preferred_element_type=F32)


def spread_lane(rows, lane):
    return jnp.broadcast_to(rows[:, lane : lane + 1], rows.shape)


def eliminate(block, panel, row):
    block = list(block)
    for step in range(0, 8, 2):
        one, two = block[step], block[step + 1]
        a, b, c = one[step : step + 1], two[step : step + 1], two[step + 1 : step + 2]
        inverse = 1.0 / (a * c - b * b)

        def reduced(rows):
            upper, lower = rows[step : step + 1], rows[step + 1 : step + 2]
            first, second = (c * upper - b * lower) * inverse, (a * lower - b * upper) * inverse
            rest = rows - (one * first + two * second)
            return jnp.where(row == step, first, jnp.where(row == step + 1, second, rest))

        panel = reduced(panel)
        block = [reduced(rows) if c >= step + 2 else rows for c, rows in enumerate(block)]
    return panel


def invert(matrix):
    matrix = list(matrix)
    count, size = len(matrix), 8 * len(matrix)
    row = lax.broadcasted_iota(jnp.int32, (8, size), 0)
    lane = lax.broadcasted_iota(jnp.int32, (8, size), 1)
    pivot = matrix[0]
    for index in range(count):
        first = 8 * index
        inside = (lane >= first) & (lane < first + 8)
        unit = jnp.where(lane == row + first, 1.0, 0.0)
        solved = eliminate([spread_lane(pivot, first + c) for c in range(8)], jnp.where(inside, unit, pivot), row)
        solved = jnp.where(inside, -solved, solved)
        update = outer_sum(jnp.where(inside, 0.0, pivot), solved)
        following = None
        if index + 1 < count:
            terms = [spread_lane(matrix[index + 1], first + c) * solved[c : c + 1] for c in range(8)]
            while len(terms) > 1:
                terms = [one + two for one, two in zip(terms[::2], terms[1::2])]
            following = jnp.where(inside, 0.0, matrix[index + 1]) - terms[0]
        for other in range(count):
            if other == index:
                matrix[other] = solved
            elif other == index + 1:
                matrix[other] = following
            else:
                matrix[other] = jnp.where(inside, 0.0, matrix[other]) - update[8 * other : 8 * other + 8]
        pivot = following
    return matrix


def solve_body(scale, centered_ref, *refs):
    *part_refs, update_ref, coeffs_ref = refs
    rows, total, lanes = centered_ref.shape
    samples = coeffs_ref.shape[1]
    summed = part_refs[0][...]
    for ref in part_refs[1:]:
        summed = summed + ref[...]
    matrix = unfold(summed)
    row_index = lax.broadcasted_iota(jnp.int32, (8, total), 0)
    lane_index = lax.broadcasted_iota(jnp.int32, (8, total), 1)
    regular = [
        matrix[first : first + 8] + jnp.where(lane_index == row_index + first, reg_shift, 0.0) for first in range(0, total, 8)
    ]
    energies = summed[total // 2 + 1 : total // 2 + 2]
    deviation = energies - jnp.sum(energies, axis=1, keepdims=True) / total
    coeffs = jnp.concatenate([-jnp.sum(part * deviation, axis=1, keepdims=True) for part in invert(regular)], axis=0)

    position = lax.axis_index("samp")
    sample = lax.broadcasted_iota(jnp.int32, (total, lanes), 0)
    lane = lax.broadcasted_iota(jnp.int32, (total, lanes), 1)
    spread = jnp.broadcast_to(coeffs, (total, lanes))
    own = jnp.sum(jnp.where(sample == lane + position * samples, spread, 0.0), axis=0, keepdims=True)
    coeffs_ref[...] = own[:, :samples]

    spread = spread * scale
    terms = [jnp.sum(centered_ref[row].astype(F32) * spread, axis=0, keepdims=True) for row in range(rows)]
    owned = rows // OFFSETS
    padded = -(-rows // 8) * 8
    table = jnp.concatenate(terms + [jnp.zeros((padded - rows, lanes), F32)], axis=0)
    row_index = lax.broadcasted_iota(jnp.int32, (padded, lanes), 0)
    for tile in range(OFFSETS):
        place = lax.broadcasted_iota(jnp.int32, (padded, lanes), 1) + tile * lanes
        picked = jnp.take_along_axis(table, place // OFFSETS, axis=1)
        for channel in range(owned):
            mask = row_index == (place % OFFSETS) * owned + channel
            update_ref[channel : channel + 1, tile * lanes : (tile + 1) * lanes] = jnp.sum(
                jnp.where(mask, picked, 0.0), axis=0, keepdims=True
            )


def far_first(members):
    return [*range(members // 2, members), *range(CORES, members // 2), *range(1, CORES)]


def swaps(x, axis, masks):
    return {mask: swap(x, axis, mask) for mask in sorted(masks, reverse=True)}


def in_order(x, axis, masks):
    blocks = {0: x, **swaps(x, axis, masks)}
    bits = lax.axis_index(axis) & functools.reduce(lambda a, b: a | b, masks)
    placed = []
    for place in sorted(blocks):
        block = blocks[0]
        for mask in sorted(masks):
            block = jnp.where(bits == place ^ mask, blocks[mask], block)
        placed.append(block)
    return jnp.concatenate(placed)


def solve_system(gram, dev_all, total):
    regular = gram + reg_shift * jnp.eye(total, dtype=F32)
    factor = jnp.linalg.cholesky(regular)
    forward = lax.linalg.triangular_solve(factor, dev_all[:, None], left_side=True, lower=True)
    return lax.linalg.triangular_solve(factor, forward, left_side=True, lower=True, transpose_a=True)[:, 0]


def local_split(activations, cotangents, energies):
    samples, layers, channels, sites = activations.shape
    owned = cotangents.shape[2]
    members = lax.axis_size("samp")
    chips = members // CORES
    total = members * samples
    position = lax.axis_index("samp")
    params_all = LAYERS * C * C * OFFSETS
    mine = owned // members
    rows = OFFSETS * mine

    own = jax.ShapeDtypeStruct((rows, samples, LANES), F32)
    block = jax.ShapeDtypeStruct((packed_rows(rows, samples), LANES), F32)
    inputs = [pltpu.with_memory_space_constraint(x, pltpu.HBM) for x in (activations, cotangents)]

    def half(far, out_shape):
        return kernel_call(
            functools.partial(grads_body, far),
            out_shape,
            [
                pltpu.VMEM(activations.shape, BF16),
                pltpu.VMEM(cotangents.shape, BF16),
                pltpu.VMEM((OFFSETS, samples * layers * owned // 2, sites), BF16),
                pltpu.VMEM((OFFSETS * owned // 2 * samples, LANES), F32),
                pltpu.SemaphoreType.DMA((2,)),
            ],
            in_specs=[pl.BlockSpec(memory_space=pltpu.HBM)] * 2,
        )(*inputs)

    far_blocks = half(True, (block,) * (members // 2))
    own, *near_blocks = half(False, (own,) + (block,) * (members // 2 - 1))
    blocks = [*near_blocks, *far_blocks]
    order = far_first(members)
    arrived = [swap(blocks[slot - 1].astype(jnp.float16), "samp", slot).astype(F32) for slot in order]

    lane = jnp.arange(total) // samples
    here = (lane == position) & (lax.axis_index("par") == 0)
    spread = jnp.where(here, jnp.tile(energies, members), 0.0)
    spread = jnp.where(jnp.arange(8)[:, None] == 1, spread[None, :], 0.0)
    centered, partial_gram = kernel_call(
        functools.partial(gram_body, total, params_all),
        (jax.ShapeDtypeStruct((rows, total, LANES), BF16), jax.ShapeDtypeStruct((total // 2 + 8, total), F32)),
    )(spread, own, *arrived)

    summed = partial_gram + swap(partial_gram, "samp", 1)
    summed = summed + sum(swaps(summed, "par", range(1, lax.axis_size("par"))).values())
    parts = [summed, *swaps(summed, "samp", range(CORES, members, CORES)).values()]
    update, local_coeffs = kernel_call(
        functools.partial(solve_body, -math.sqrt(params_all / total)),
        (jax.ShapeDtypeStruct((mine, OFFSETS * LANES), F32), jax.ShapeDtypeStruct((1, samples), F32)),
    )(centered, *parts)
    update = in_order(update, "samp", range(1, CORES))
    update = in_order(update, "samp", range(CORES, members, CORES))
    return update, local_coeffs[0]


def local_gather(activations, cotangents, energies):
    samples, layers, channels, sites = activations.shape
    owned = cotangents.shape[2]
    position = lax.axis_index("samp")
    total = lax.axis_size("samp") * samples
    params_all = LAYERS * C * C * OFFSETS
    field = cotangents.reshape(samples, layers, owned, SIDE, SIDE)
    shifted = [jnp.roll(field, (row - 1, col - 1), axis=(3, 4)) for row in range(3) for col in range(3)]
    stacked = jnp.stack(shifted, axis=3).reshape(samples, layers, owned * OFFSETS, sites)
    grads = jnp.einsum("slkx,slix->slki", stacked, activations, preferred_element_type=F32)
    grads = grads.reshape(samples, layers, owned, OFFSETS, channels).transpose(0, 2, 1, 4, 3)
    grads = grads.reshape(samples, owned * layers * channels * OFFSETS)
    col_sums, energy_sum = lax.psum((jnp.sum(grads, axis=0), jnp.sum(energies)), "samp")
    centered = ((grads - col_sums / total) * (1.0 / math.sqrt(params_all))).astype(BF16)
    everyone = lax.all_gather(centered, "samp", axis=0, tiled=True)
    partial_gram = lax.dot_general(centered, everyone, (((1,), (1,)), ((), ())), preferred_element_type=F32)
    gram = lax.all_gather(lax.psum(partial_gram, "par"), "samp", axis=0, tiled=True)
    deviation = lax.all_gather(energies - energy_sum / total, "samp", axis=0, tiled=True)
    coeffs = solve_system(gram, deviation, total)
    local_coeffs = lax.dynamic_slice_in_dim(coeffs, position * samples, samples)
    term = jnp.dot(local_coeffs[None, :], centered.astype(F32), precision=lax.Precision.HIGHEST)[0]
    update = -math.sqrt(params_all / total) * lax.psum(term, "samp")
    return update.reshape(owned, -1), local_coeffs


def local(activations, cotangents, energies):
    if cotangents.shape[2] % lax.axis_size("samp"):
        return local_gather(activations, cotangents, energies)
    return local_split(activations, cotangents, energies)


def solution(mesh):
    return jax.shard_map(
        local,
        mesh=mesh,
        in_specs=(P("samp", None, None, None), P("samp", None, "par", None), P("samp")),
        out_specs=(P("par", None), P("samp")),
        check_vma=False,
    )
```

```python
import functools
import math

import jax
import jax.numpy as jnp
from jax import lax
from jax.experimental import pallas as pl
from jax.experimental.pallas import tpu as pltpu
from jax.sharding import PartitionSpec as P

C = 64
SIDE = 16
LAYERS = 2
SITES = SIDE * SIDE
OFFSETS = 9
LANES = 128
CORES = 2


reg_shift = 0.1
F32 = jnp.float32
BF16 = jnp.bfloat16
VMEM_LIMIT = 48 * 1024 * 1024


def kernel_call(body, out_shape, scratch_shapes=(), **options):
    return pl.pallas_call(
        body,
        out_shape=out_shape,
        **options,
        scratch_shapes=scratch_shapes,
        compiler_params=pltpu.CompilerParams(vmem_limit_bytes=VMEM_LIMIT),
    )


def swap(x, axis, mask):
    count = lax.axis_size(axis)
    return lax.ppermute(x, axis, [(i, i ^ mask) for i in range(count)])


def exponent(values):
    top = jnp.maximum(jnp.max(jnp.abs(values), axis=0, keepdims=True), 1e-30)
    return 14.0 - jnp.floor(jnp.log2(top))


def packed_rows(rows, samples):
    return -(-(rows * samples + rows + 2) // 8) * 8


def grads_body(far, acts_hbm, cots_hbm, *refs):
    *out_refs, acts_ref, cots_ref, shifted_ref, grads_ref, semaphores = refs
    copies = [
        pltpu.make_async_copy(cots_hbm, cots_ref, semaphores.at[0]),
        pltpu.make_async_copy(acts_hbm, acts_ref, semaphores.at[1]),
    ]
    for copy in copies:
        copy.start()
    samples, layers, owned, sites = cots_ref.shape
    members = len(out_refs)
    owned = owned // 2
    mine = owned // members
    rows = OFFSETS * mine
    moves = []
    source = lax.broadcasted_iota(jnp.int32, (sites, sites), 0)
    target = lax.broadcasted_iota(jnp.int32, (1, sites), 1)
    for offset in range(OFFSETS):
        row, col = target // SIDE, target % SIDE
        row = (row + SIDE - (offset // 3 - 1)) % SIDE
        col = (col + SIDE - (offset % 3 - 1)) % SIDE
        moves.append(jnp.where(source == row * SIDE + col, 1.0, 0.0).astype(BF16))
    position = lax.axis_index("samp")
    upper = (position // members + int(far)) % 2 == 1
    copies[0].wait()
    field = cots_ref[...].astype(F32).reshape(samples * layers, 2, owned, sites)
    field = jnp.where(upper, field[:, 1], field[:, 0]).reshape(samples * layers * owned, sites).astype(BF16)
    for offset in range(OFFSETS):
        shifted_ref[offset] = jnp.dot(field, moves[offset], preferred_element_type=F32).astype(BF16)
    copies[1].wait()
    lanes = grads_ref.shape[1]
    lane = lax.broadcasted_iota(jnp.int32, (OFFSETS, owned, lanes), 2)
    for sample in range(samples):
        first = sample * layers * owned
        left = jnp.concatenate([shifted_ref[k, first : first + layers * owned, :] for k in range(OFFSETS)], axis=0)
        right = acts_ref[sample].reshape(layers * C, sites)
        products = lax.dot_general(left, right, (((1,), (1,)), ((), ())), preferred_element_type=F32)
        products = products.reshape(OFFSETS, layers, owned, lanes)
        grads = products[:, 0]
        for layer in range(1, layers):
            grads = jnp.where(lane >= layer * C, products[:, layer], grads)
        grads_ref[pl.ds(sample, OFFSETS * owned, stride=samples), :] = grads.reshape(OFFSETS * owned, lanes)
    for index in range(members):
        slot = index + members * int(far)
        start = ((position ^ slot) % members) * (mine * samples)
        pieces = [
            grads_ref[pl.ds(pl.multiple_of(k * owned * samples + start, mine * samples), mine * samples), :] for k in range(OFFSETS)
        ]
        values = jnp.concatenate(pieces, axis=0).reshape(rows, samples, lanes)
        values_ref = out_refs[index]
        if slot == 0:
            values_ref[...] = values
            continue
        reference = (jnp.sum(values, axis=1) * (1.0 / samples)).astype(BF16).astype(F32)
        values = values - reference[:, None, :]
        shift = exponent(jnp.max(jnp.abs(values), axis=0))
        reference_shift = exponent(reference)
        last = rows * samples
        values_ref[0:last, :] = (values * jnp.exp2(shift)).reshape(last, lanes)
        values_ref[last : last + rows, :] = reference * jnp.exp2(reference_shift)
        values_ref[last + rows : last + rows + 1, :] = shift
        values_ref[last + rows + 1 : last + rows + 2, :] = reference_shift
        spare = values_ref.shape[0] - (last + rows + 2)
        if spare:
            values_ref[last + rows + 2 :, :] = jnp.zeros((spare, lanes), F32)


def halves(half):
    row = lax.broadcasted_iota(jnp.int32, (half, 2 * half), 0)
    lane = lax.broadcasted_iota(jnp.int32, (half, 2 * half), 1)
    return row, lane


def fold(matrix, energies):
    half = matrix.shape[0] // 2
    row, lane = halves(half)
    top, bottom = matrix[:half], matrix[half:]
    turned = pltpu.roll(bottom, half, 1)
    diagonal = jnp.sum(jnp.where(lane == row, turned, 0.0), axis=0, keepdims=True)
    first = lax.broadcasted_iota(jnp.int32, energies.shape, 0) == 0
    rest = jnp.where(first, diagonal, energies)
    return jnp.concatenate([jnp.where((lane > row) & (lane < half), turned, top), rest], axis=0)


def unfold(folded):
    half = folded.shape[1] // 2
    row, lane = halves(half)
    body, diagonal = folded[:half], folded[half : half + 1]
    flipped = body.T
    mixed, crossed = flipped[:half], flipped[half:]
    both = jnp.concatenate([mixed, crossed], axis=1)
    top = jnp.where((lane > row) & (lane < half), both, body)
    lower = jnp.concatenate([crossed, mixed], axis=1)
    turned = pltpu.roll(body, half, 1)
    place = lane - half
    corner = jnp.where(place > row, turned, jnp.where(place == row, pltpu.roll(jnp.broadcast_to(diagonal, turned.shape), half, 1), lower))
    return jnp.concatenate([top, jnp.where(lane < half, lower, corner)], axis=0)


def gram_body(total, params_all, energies_ref, own_ref, *refs):
    rows, group, lanes = own_ref.shape
    *value_refs, centered_ref, gram_ref = refs
    by_slot = dict(zip(far_first(len(value_refs) + 1), value_refs))
    value_refs = [by_slot[slot] for slot in sorted(by_slot)]
    position = lax.axis_index("samp")
    gram = jnp.zeros((total, total), F32)
    last = rows * group
    scales = [jnp.exp2(-ref[last + rows : last + rows + 1, :]) for ref in value_refs]
    references = [ref[last : last + rows, :] * jnp.exp2(-ref[last + rows + 1 : last + rows + 2, :]) for ref in value_refs]
    pair = []
    for row in range(rows):
        blocks = [own_ref[row]]
        for ref, scale, reference in zip(value_refs, scales, references):
            blocks.append(ref[row * group : (row + 1) * group, :] * scale + reference[row : row + 1, :])
        mean = sum(jnp.sum(block, axis=0, keepdims=True) for block in blocks) / total
        for slot in range(len(blocks)):
            place = pl.ds(pl.multiple_of((position ^ slot) * group, group), group)
            centered_ref[row, place, :] = ((blocks[slot] - mean) * (1.0 / math.sqrt(params_all))).astype(BF16)
        pair.append(centered_ref[row])
        if len(pair) == 2 or row == rows - 1:
            both = jnp.concatenate(pair, axis=1)
            gram = gram + lax.dot_general(both, both, (((1,), (1,)), ((), ())), preferred_element_type=F32)
            pair = []
    gram_ref[...] = fold(gram, energies_ref[...])


def thirds(values):
    high = values.astype(BF16).astype(F32)
    middle = (values - high).astype(BF16).astype(F32)
    return high, middle, values - high - middle


def outer_sum(left, right):
    a, b, c = thirds(left)
    d, e, f = thirds(right)
    lefts = jnp.concatenate([a, a, b, a, b, c], axis=0).astype(BF16)
    rights = jnp.concatenate([d, e, d, f, e, d], axis=0).astype(BF16)
    return lax.dot_general(lefts, rights, (((0,), (0,)), ((), ())), preferred_element_type=F32)


def spread_lane(rows, lane):
    return jnp.broadcast_to(rows[:, lane : lane + 1], rows.shape)


def eliminate(block, panel, row):
    block = list(block)
    for step in range(0, 8, 2):
        one, two = block[step], block[step + 1]
        a, b, c = one[step : step + 1], two[step : step + 1], two[step + 1 : step + 2]
        inverse = 1.0 / (a * c - b * b)

        def reduced(rows):
            upper, lower = rows[step : step + 1], rows[step + 1 : step + 2]
            first, second = (c * upper - b * lower) * inverse, (a * lower - b * upper) * inverse
            rest = rows - (one * first + two * second)
            return jnp.where(row == step, first, jnp.where(row == step + 1, second, rest))

        panel = reduced(panel)
        block = [reduced(rows) if c >= step + 2 else rows for c, rows in enumerate(block)]
    return panel


def invert(matrix):
    matrix = list(matrix)
    count, size = len(matrix), 8 * len(matrix)
    row = lax.broadcasted_iota(jnp.int32, (8, size), 0)
    lane = lax.broadcasted_iota(jnp.int32, (8, size), 1)
    pivot = matrix[0]
    for index in range(count):
        first = 8 * index
        inside = (lane >= first) & (lane < first + 8)
        unit = jnp.where(lane == row + first, 1.0, 0.0)
        solved = eliminate([spread_lane(pivot, first + c) for c in range(8)], jnp.where(inside, unit, pivot), row)
        solved = jnp.where(inside, -solved, solved)
        update = outer_sum(jnp.where(inside, 0.0, pivot), solved)
        following = None
        if index + 1 < count:
            terms = [spread_lane(matrix[index + 1], first + c) * solved[c : c + 1] for c in range(8)]
            while len(terms) > 1:
                terms = [one + two for one, two in zip(terms[::2], terms[1::2])]
            following = jnp.where(inside, 0.0, matrix[index + 1]) - terms[0]
        for other in range(count):
            if other == index:
                matrix[other] = solved
            elif other == index + 1:
                matrix[other] = following
            else:
                matrix[other] = jnp.where(inside, 0.0, matrix[other]) - update[8 * other : 8 * other + 8]
        pivot = following
    return matrix


def arrange(terms):
    rows, lanes = len(terms), terms[0].shape[1]
    owned = rows // OFFSETS
    padded = -(-rows // 8) * 8
    table = jnp.concatenate(terms + [jnp.zeros((padded - rows, lanes), F32)], axis=0)
    row_index = lax.broadcasted_iota(jnp.int32, (padded, lanes), 0)
    tiles = []
    for tile in range(OFFSETS):
        place = lax.broadcasted_iota(jnp.int32, (padded, lanes), 1) + tile * lanes
        picked = jnp.take_along_axis(table, place // OFFSETS, axis=1)
        sums = []
        for channel in range(owned):
            mask = row_index == (place % OFFSETS) * owned + channel
            sums.append(jnp.sum(jnp.where(mask, picked, 0.0), axis=0, keepdims=True))
        tiles.append(jnp.concatenate(sums, axis=0))
    return jnp.concatenate(tiles, axis=1)


def solve_body(scale, centered_ref, across_ref, *refs):
    *part_refs, update_ref, coeffs_ref = refs
    rows, total, lanes = centered_ref.shape
    samples = coeffs_ref.shape[1]
    summed = part_refs[0][...]
    for ref in part_refs[1:]:
        summed = summed + ref[...]
    matrix = unfold(summed)
    row_index = lax.broadcasted_iota(jnp.int32, (8, total), 0)
    lane_index = lax.broadcasted_iota(jnp.int32, (8, total), 1)
    regular = [
        matrix[first : first + 8] + jnp.where(lane_index == row_index + first, reg_shift, 0.0) for first in range(0, total, 8)
    ]
    energies = summed[total // 2 + 1 : total // 2 + 2]
    deviation = energies - jnp.sum(energies, axis=1, keepdims=True) / total
    coeffs = jnp.concatenate([-jnp.sum(part * deviation, axis=1, keepdims=True) for part in invert(regular)], axis=0)

    position = lax.axis_index("samp")
    sample = lax.broadcasted_iota(jnp.int32, (total, lanes), 0)
    lane = lax.broadcasted_iota(jnp.int32, (total, lanes), 1)
    spread = jnp.broadcast_to(coeffs, (total, lanes))
    own = jnp.sum(jnp.where(sample == lane + position * samples, spread, 0.0), axis=0, keepdims=True)
    coeffs_ref[...] = own[:, :samples]

    spread = spread * scale
    own, across = (
        arrange([jnp.sum(ref[row].astype(F32) * spread, axis=0, keepdims=True) for row in range(rows)])
        for ref in (centered_ref, across_ref)
    )
    even = position % CORES == 0
    owned = own.shape[0]
    update_ref[0:owned, :] = jnp.where(even, own, across)
    update_ref[owned : 2 * owned, :] = jnp.where(even, across, own)


def far_first(members):
    return [*range(members // 2, members), *range(CORES, members // 2), *range(1, CORES)]


def swaps(x, axis, masks):
    return {mask: swap(x, axis, mask) for mask in sorted(masks, reverse=True)}


def in_order(x, axis, masks):
    blocks = {0: x, **swaps(x, axis, masks)}
    bits = lax.axis_index(axis) & functools.reduce(lambda a, b: a | b, masks)
    placed = []
    for place in sorted(blocks):
        block = blocks[0]
        for mask in sorted(masks):
            block = jnp.where(bits == place ^ mask, blocks[mask], block)
        placed.append(block)
    return jnp.concatenate(placed)


def solve_system(gram, dev_all, total):
    regular = gram + reg_shift * jnp.eye(total, dtype=F32)
    factor = jnp.linalg.cholesky(regular)
    forward = lax.linalg.triangular_solve(factor, dev_all[:, None], left_side=True, lower=True)
    return lax.linalg.triangular_solve(factor, forward, left_side=True, lower=True, transpose_a=True)[:, 0]


def local_split(activations, cotangents, energies):
    samples, layers, channels, sites = activations.shape
    owned = cotangents.shape[2]
    members = lax.axis_size("samp")
    chips = members // CORES
    total = members * samples
    position = lax.axis_index("samp")
    params_all = LAYERS * C * C * OFFSETS
    mine = owned // members
    rows = OFFSETS * mine

    own = jax.ShapeDtypeStruct((rows, samples, LANES), F32)
    block = jax.ShapeDtypeStruct((packed_rows(rows, samples), LANES), F32)
    inputs = [pltpu.with_memory_space_constraint(x, pltpu.HBM) for x in (activations, cotangents)]

    def half(far, out_shape):
        return kernel_call(
            functools.partial(grads_body, far),
            out_shape,
            [
                pltpu.VMEM(activations.shape, BF16),
                pltpu.VMEM(cotangents.shape, BF16),
                pltpu.VMEM((OFFSETS, samples * layers * owned // 2, sites), BF16),
                pltpu.VMEM((OFFSETS * owned // 2 * samples, LANES), F32),
                pltpu.SemaphoreType.DMA((2,)),
            ],
            in_specs=[pl.BlockSpec(memory_space=pltpu.HBM)] * 2,
        )(*inputs)

    far_blocks = half(True, (block,) * (members // 2))
    own, *near_blocks = half(False, (own,) + (block,) * (members // 2 - 1))
    blocks = [*near_blocks, *far_blocks]
    order = far_first(members)
    arrived = [swap(blocks[slot - 1].astype(jnp.float16), "samp", slot).astype(F32) for slot in order]

    lane = jnp.arange(total) // samples
    here = (lane == position) & (lax.axis_index("par") == 0)
    spread = jnp.where(here, jnp.tile(energies, members), 0.0)
    spread = jnp.where(jnp.arange(8)[:, None] == 1, spread[None, :], 0.0)
    centered, partial_gram = kernel_call(
        functools.partial(gram_body, total, params_all),
        (jax.ShapeDtypeStruct((rows, total, LANES), BF16), jax.ShapeDtypeStruct((total // 2 + 8, total), F32)),
    )(spread, own, *arrived)

    summed = partial_gram + swap(partial_gram, "samp", 1)
    ready, summed = lax.optimization_barrier((centered, summed))
    across = swap(ready, "samp", 1)
    masks = [*range(2, lax.axis_size("par")), 1]
    summed = sum((swap(summed, "par", mask) for mask in masks), start=summed)
    parts = [summed, *swaps(summed, "samp", range(CORES, members, CORES)).values()]
    update, local_coeffs = kernel_call(
        functools.partial(solve_body, -math.sqrt(params_all / total)),
        (jax.ShapeDtypeStruct((CORES * mine, OFFSETS * LANES), F32), jax.ShapeDtypeStruct((1, samples), F32)),
    )(centered, across, *parts)
    update = in_order(update, "samp", range(CORES, members, CORES))
    return update, local_coeffs[0]


def local_gather(activations, cotangents, energies):
    samples, layers, channels, sites = activations.shape
    owned = cotangents.shape[2]
    position = lax.axis_index("samp")
    total = lax.axis_size("samp") * samples
    params_all = LAYERS * C * C * OFFSETS
    field = cotangents.reshape(samples, layers, owned, SIDE, SIDE)
    shifted = [jnp.roll(field, (row - 1, col - 1), axis=(3, 4)) for row in range(3) for col in range(3)]
    stacked = jnp.stack(shifted, axis=3).reshape(samples, layers, owned * OFFSETS, sites)
    grads = jnp.einsum("slkx,slix->slki", stacked, activations, preferred_element_type=F32)
    grads = grads.reshape(samples, layers, owned, OFFSETS, channels).transpose(0, 2, 1, 4, 3)
    grads = grads.reshape(samples, owned * layers * channels * OFFSETS)
    col_sums, energy_sum = lax.psum((jnp.sum(grads, axis=0), jnp.sum(energies)), "samp")
    centered = ((grads - col_sums / total) * (1.0 / math.sqrt(params_all))).astype(BF16)
    everyone = lax.all_gather(centered, "samp", axis=0, tiled=True)
    partial_gram = lax.dot_general(centered, everyone, (((1,), (1,)), ((), ())), preferred_element_type=F32)
    gram = lax.all_gather(lax.psum(partial_gram, "par"), "samp", axis=0, tiled=True)
    deviation = lax.all_gather(energies - energy_sum / total, "samp", axis=0, tiled=True)
    coeffs = solve_system(gram, deviation, total)
    local_coeffs = lax.dynamic_slice_in_dim(coeffs, position * samples, samples)
    term = jnp.dot(local_coeffs[None, :], centered.astype(F32), precision=lax.Precision.HIGHEST)[0]
    update = -math.sqrt(params_all / total) * lax.psum(term, "samp")
    return update.reshape(owned, -1), local_coeffs


def local(activations, cotangents, energies):
    if cotangents.shape[2] % lax.axis_size("samp"):
        return local_gather(activations, cotangents, energies)
    return local_split(activations, cotangents, energies)


def solution(mesh):
    return jax.shard_map(
        local,
        mesh=mesh,
        in_specs=(P("samp", None, None, None), P("samp", None, "par", None), P("samp")),
        out_specs=(P("par", None), P("samp")),
        check_vma=False,
    )
```

```python
import functools
import math

import jax
import jax.numpy as jnp
from jax import lax
from jax.experimental import pallas as pl
from jax.experimental.pallas import tpu as pltpu
from jax.sharding import PartitionSpec as P

C = 64
SIDE = 16
LAYERS = 2
SITES = SIDE * SIDE
OFFSETS = 9
LANES = 128
CORES = 2


reg_shift = 0.1
F32 = jnp.float32
BF16 = jnp.bfloat16
VMEM_LIMIT = 48 * 1024 * 1024


def kernel_call(body, out_shape, scratch_shapes=(), **options):
    return pl.pallas_call(
        body,
        out_shape=out_shape,
        **options,
        scratch_shapes=scratch_shapes,
        compiler_params=pltpu.CompilerParams(vmem_limit_bytes=VMEM_LIMIT),
    )


def swap(x, axis, mask):
    count = lax.axis_size(axis)
    return lax.ppermute(x, axis, [(i, i ^ mask) for i in range(count)])


def exponent(values):
    top = jnp.maximum(jnp.max(jnp.abs(values), axis=0, keepdims=True), 1e-30)
    return 14.0 - jnp.floor(jnp.log2(top))


def packed_rows(rows, samples):
    return -(-(rows * samples + rows + 2) // 8) * 8


def grads_body(far, acts_hbm, cots_hbm, *refs):
    *out_refs, acts_ref, cots_ref, shifted_ref, grads_ref, semaphores = refs
    copies = [
        pltpu.make_async_copy(cots_hbm, cots_ref, semaphores.at[0]),
        pltpu.make_async_copy(acts_hbm, acts_ref, semaphores.at[1]),
    ]
    for copy in copies:
        copy.start()
    samples, layers, owned, sites = cots_ref.shape
    members = len(out_refs)
    owned = owned // 2
    mine = owned // members
    rows = OFFSETS * mine
    moves = []
    source = lax.broadcasted_iota(jnp.int32, (sites, sites), 0)
    target = lax.broadcasted_iota(jnp.int32, (1, sites), 1)
    for offset in range(OFFSETS):
        row, col = target // SIDE, target % SIDE
        row = (row + SIDE - (offset // 3 - 1)) % SIDE
        col = (col + SIDE - (offset % 3 - 1)) % SIDE
        moves.append(jnp.where(source == row * SIDE + col, 1.0, 0.0).astype(BF16))
    position = lax.axis_index("samp")
    upper = (position // members + int(far)) % 2 == 1
    copies[0].wait()
    field = cots_ref[...].astype(F32).reshape(samples * layers, 2, owned, sites)
    field = jnp.where(upper, field[:, 1], field[:, 0]).reshape(samples * layers * owned, sites).astype(BF16)
    for offset in range(OFFSETS):
        shifted_ref[offset] = jnp.dot(field, moves[offset], preferred_element_type=F32).astype(BF16)
    copies[1].wait()
    lanes = grads_ref.shape[1]
    lane = lax.broadcasted_iota(jnp.int32, (OFFSETS, owned, lanes), 2)
    for sample in range(samples):
        first = sample * layers * owned
        left = jnp.concatenate([shifted_ref[k, first : first + layers * owned, :] for k in range(OFFSETS)], axis=0)
        right = acts_ref[sample].reshape(layers * C, sites)
        products = lax.dot_general(left, right, (((1,), (1,)), ((), ())), preferred_element_type=F32)
        products = products.reshape(OFFSETS, layers, owned, lanes)
        grads = products[:, 0]
        for layer in range(1, layers):
            grads = jnp.where(lane >= layer * C, products[:, layer], grads)
        grads_ref[pl.ds(sample, OFFSETS * owned, stride=samples), :] = grads.reshape(OFFSETS * owned, lanes)
    for index in range(members):
        slot = index + members * int(far)
        start = ((position ^ slot) % members) * (mine * samples)
        pieces = [
            grads_ref[pl.ds(pl.multiple_of(k * owned * samples + start, mine * samples), mine * samples), :] for k in range(OFFSETS)
        ]
        values = jnp.concatenate(pieces, axis=0).reshape(rows, samples, lanes)
        values_ref = out_refs[index]
        if slot == 0:
            values_ref[...] = values
            continue
        reference = (jnp.sum(values, axis=1) * (1.0 / samples)).astype(BF16).astype(F32)
        values = values - reference[:, None, :]
        shift = exponent(jnp.max(jnp.abs(values), axis=0))
        reference_shift = exponent(reference)
        last = rows * samples
        values_ref[0:last, :] = (values * jnp.exp2(shift)).reshape(last, lanes)
        values_ref[last : last + rows, :] = reference * jnp.exp2(reference_shift)
        values_ref[last + rows : last + rows + 1, :] = shift
        values_ref[last + rows + 1 : last + rows + 2, :] = reference_shift
        spare = values_ref.shape[0] - (last + rows + 2)
        if spare:
            values_ref[last + rows + 2 :, :] = jnp.zeros((spare, lanes), F32)


def halves(half):
    row = lax.broadcasted_iota(jnp.int32, (half, 2 * half), 0)
    lane = lax.broadcasted_iota(jnp.int32, (half, 2 * half), 1)
    return row, lane


def fold(matrix, energies):
    half = matrix.shape[0] // 2
    row, lane = halves(half)
    top, bottom = matrix[:half], matrix[half:]
    turned = pltpu.roll(bottom, half, 1)
    diagonal = jnp.sum(jnp.where(lane == row, turned, 0.0), axis=0, keepdims=True)
    first = lax.broadcasted_iota(jnp.int32, energies.shape, 0) == 0
    rest = jnp.where(first, diagonal, energies)
    return jnp.concatenate([jnp.where((lane > row) & (lane < half), turned, top), rest], axis=0)


def unfold(folded):
    half = folded.shape[1] // 2
    row, lane = halves(half)
    body, diagonal = folded[:half], folded[half : half + 1]
    flipped = body.T
    mixed, crossed = flipped[:half], flipped[half:]
    both = jnp.concatenate([mixed, crossed], axis=1)
    top = jnp.where((lane > row) & (lane < half), both, body)
    lower = jnp.concatenate([crossed, mixed], axis=1)
    turned = pltpu.roll(body, half, 1)
    place = lane - half
    corner = jnp.where(place > row, turned, jnp.where(place == row, pltpu.roll(jnp.broadcast_to(diagonal, turned.shape), half, 1), lower))
    return jnp.concatenate([top, jnp.where(lane < half, lower, corner)], axis=0)


def gram_body(total, params_all, energies_ref, own_ref, *refs):
    rows, group, lanes = own_ref.shape
    *value_refs, centered_ref, gram_ref = refs
    by_slot = dict(zip(far_first(len(value_refs) + 1), value_refs))
    value_refs = [by_slot[slot] for slot in sorted(by_slot)]
    position = lax.axis_index("samp")
    gram = jnp.zeros((total, total), F32)
    last = rows * group
    scales = [jnp.exp2(-ref[last + rows : last + rows + 1, :]) for ref in value_refs]
    references = [ref[last : last + rows, :] * jnp.exp2(-ref[last + rows + 1 : last + rows + 2, :]) for ref in value_refs]
    pair = []
    for row in range(rows):
        blocks = [own_ref[row]]
        for ref, scale, reference in zip(value_refs, scales, references):
            blocks.append(ref[row * group : (row + 1) * group, :] * scale + reference[row : row + 1, :])
        mean = sum(jnp.sum(block, axis=0, keepdims=True) for block in blocks) / total
        for slot in range(len(blocks)):
            place = pl.ds(pl.multiple_of((position ^ slot) * group, group), group)
            centered_ref[row, place, :] = ((blocks[slot] - mean) * (1.0 / math.sqrt(params_all))).astype(BF16)
        pair.append(centered_ref[row])
        if len(pair) == 2 or row == rows - 1:
            both = jnp.concatenate(pair, axis=1)
            gram = gram + lax.dot_general(both, both, (((1,), (1,)), ((), ())), preferred_element_type=F32)
            pair = []
    gram_ref[...] = fold(gram, energies_ref[...])


WIDTH = 16


def thirds(values):
    high = values.astype(BF16)
    rest = values - high.astype(F32)
    middle = rest.astype(BF16)
    return high, middle, (rest - middle.astype(F32)).astype(BF16)


def outer_sum(left, right):
    a, b, c = thirds(left)
    d, e, f = thirds(right)
    lefts = jnp.concatenate([a, a, b, a, b, c], axis=0)
    rights = jnp.concatenate([d, e, d, f, e, d], axis=0)
    return lax.dot_general(lefts, rights, (((0,), (0,)), ((), ())), preferred_element_type=F32)


def spread_lane(rows, lane):
    return jnp.broadcast_to(rows[:, lane : lane + 1], rows.shape)


def eliminate(block, panel, row):
    block = list(block)
    for step in range(0, len(block), 2):
        one, two = block[step], block[step + 1]
        a, b, c = one[step : step + 1], two[step : step + 1], two[step + 1 : step + 2]
        inverse = 1.0 / (a * c - b * b)
        upper_row, lower_row = row == step, row == step + 1
        done = upper_row | lower_row
        one = jnp.where(done, jnp.where(upper_row, -1.0, 0.0), one)
        two = jnp.where(done, jnp.where(lower_row, -1.0, 0.0), two)

        def reduced(rows):
            upper, lower = rows[step : step + 1], rows[step + 1 : step + 2]
            first, second = (c * upper - b * lower) * inverse, (a * lower - b * upper) * inverse
            return jnp.where(done, 0.0, rows) - (one * first + two * second)

        panel = reduced(panel)
        block = [reduced(rows) if c >= step + 2 else rows for c, rows in enumerate(block)]
    return panel


def invert(matrix):
    matrix = list(matrix)
    count, size = len(matrix), WIDTH * len(matrix)
    row = lax.broadcasted_iota(jnp.int32, (WIDTH, size), 0)
    lane = lax.broadcasted_iota(jnp.int32, (WIDTH, size), 1)
    pivot = matrix[0]
    for index in range(count):
        first = WIDTH * index
        inside = (lane >= first) & (lane < first + WIDTH)
        unit = jnp.where(lane == row + first, 1.0, 0.0)
        solved = eliminate([spread_lane(pivot, first + c) for c in range(WIDTH)], jnp.where(inside, unit, pivot), row)
        solved = jnp.where(inside, -solved, solved)
        update = outer_sum(jnp.where(inside, 0.0, pivot), solved)
        following = None
        if index + 1 < count:
            terms = [spread_lane(matrix[index + 1], first + c) * solved[c : c + 1] for c in range(WIDTH)]
            following = jnp.where(inside, 0.0, matrix[index + 1])
            for term in terms:
                following = following - term
        for other in range(count):
            if other == index:
                matrix[other] = solved
            elif other == index + 1:
                matrix[other] = following
            else:
                matrix[other] = jnp.where(inside, 0.0, matrix[other]) - update[WIDTH * other : WIDTH * (other + 1)]
        pivot = following
    return matrix


def arrange(terms):
    rows, lanes = len(terms), terms[0].shape[1]
    owned = rows // OFFSETS
    padded = -(-rows // 8) * 8
    table = jnp.concatenate(terms + [jnp.zeros((padded - rows, lanes), F32)], axis=0)
    row_index = lax.broadcasted_iota(jnp.int32, (padded, lanes), 0)
    tiles = []
    for tile in range(OFFSETS):
        place = lax.broadcasted_iota(jnp.int32, (padded, lanes), 1) + tile * lanes
        picked = jnp.take_along_axis(table, place // OFFSETS, axis=1)
        sums = []
        for channel in range(owned):
            mask = row_index == (place % OFFSETS) * owned + channel
            sums.append(jnp.sum(jnp.where(mask, picked, 0.0), axis=0, keepdims=True))
        tiles.append(jnp.concatenate(sums, axis=0))
    return jnp.concatenate(tiles, axis=1)


def solve_body(scale, centered_ref, across_ref, *refs):
    *part_refs, update_ref, coeffs_ref = refs
    rows, total, lanes = centered_ref.shape
    samples = coeffs_ref.shape[1]
    summed = part_refs[0][...]
    for ref in part_refs[1:]:
        summed = summed + ref[...]
    matrix = unfold(summed)
    row_index = lax.broadcasted_iota(jnp.int32, (WIDTH, total), 0)
    lane_index = lax.broadcasted_iota(jnp.int32, (WIDTH, total), 1)
    regular = [
        matrix[first : first + WIDTH] + jnp.where(lane_index == row_index + first, reg_shift, 0.0)
        for first in range(0, total, WIDTH)
    ]
    energies = summed[total // 2 + 1 : total // 2 + 2]
    deviation = energies - jnp.sum(energies, axis=1, keepdims=True) / total
    coeffs = jnp.concatenate([-jnp.sum(part * deviation, axis=1, keepdims=True) for part in invert(regular)], axis=0)

    position = lax.axis_index("samp")
    sample = lax.broadcasted_iota(jnp.int32, (total, lanes), 0)
    lane = lax.broadcasted_iota(jnp.int32, (total, lanes), 1)
    spread = jnp.broadcast_to(coeffs, (total, lanes))
    own = jnp.sum(jnp.where(sample == lane + position * samples, spread, 0.0), axis=0, keepdims=True)
    coeffs_ref[...] = own[:, :samples]

    spread = spread * scale
    own, across = (
        arrange([jnp.sum(ref[row].astype(F32) * spread, axis=0, keepdims=True) for row in range(rows)])
        for ref in (centered_ref, across_ref)
    )
    even = position % CORES == 0
    owned = own.shape[0]
    update_ref[0:owned, :] = jnp.where(even, own, across)
    update_ref[owned : 2 * owned, :] = jnp.where(even, across, own)


def far_first(members):
    return [*range(members // 2, members), *range(CORES, members // 2), *range(1, CORES)]


def swaps(x, axis, masks):
    return {mask: swap(x, axis, mask) for mask in sorted(masks, reverse=True)}


def in_order(x, axis, masks):
    blocks = {0: x, **swaps(x, axis, masks)}
    bits = lax.axis_index(axis) & functools.reduce(lambda a, b: a | b, masks)
    placed = []
    for place in sorted(blocks):
        block = blocks[0]
        for mask in sorted(masks):
            block = jnp.where(bits == place ^ mask, blocks[mask], block)
        placed.append(block)
    return jnp.concatenate(placed)


def solve_system(gram, dev_all, total):
    regular = gram + reg_shift * jnp.eye(total, dtype=F32)
    factor = jnp.linalg.cholesky(regular)
    forward = lax.linalg.triangular_solve(factor, dev_all[:, None], left_side=True, lower=True)
    return lax.linalg.triangular_solve(factor, forward, left_side=True, lower=True, transpose_a=True)[:, 0]


def local_split(activations, cotangents, energies):
    samples, layers, channels, sites = activations.shape
    owned = cotangents.shape[2]
    members = lax.axis_size("samp")
    chips = members // CORES
    total = members * samples
    position = lax.axis_index("samp")
    params_all = LAYERS * C * C * OFFSETS
    mine = owned // members
    rows = OFFSETS * mine

    own = jax.ShapeDtypeStruct((rows, samples, LANES), F32)
    block = jax.ShapeDtypeStruct((packed_rows(rows, samples), LANES), F32)
    inputs = [pltpu.with_memory_space_constraint(x, pltpu.HBM) for x in (activations, cotangents)]

    def half(far, out_shape):
        return kernel_call(
            functools.partial(grads_body, far),
            out_shape,
            [
                pltpu.VMEM(activations.shape, BF16),
                pltpu.VMEM(cotangents.shape, BF16),
                pltpu.VMEM((OFFSETS, samples * layers * owned // 2, sites), BF16),
                pltpu.VMEM((OFFSETS * owned // 2 * samples, LANES), F32),
                pltpu.SemaphoreType.DMA((2,)),
            ],
            in_specs=[pl.BlockSpec(memory_space=pltpu.HBM)] * 2,
        )(*inputs)

    far_blocks = half(True, (block,) * (members // 2))
    own, *near_blocks = half(False, (own,) + (block,) * (members // 2 - 1))
    blocks = [*near_blocks, *far_blocks]
    order = far_first(members)
    arrived = [swap(blocks[slot - 1].astype(jnp.float16), "samp", slot).astype(F32) for slot in order]

    lane = jnp.arange(total) // samples
    here = (lane == position) & (lax.axis_index("par") == 0)
    spread = jnp.where(here, jnp.tile(energies, members), 0.0)
    spread = jnp.where(jnp.arange(8)[:, None] == 1, spread[None, :], 0.0)
    centered, partial_gram = kernel_call(
        functools.partial(gram_body, total, params_all),
        (jax.ShapeDtypeStruct((rows, total, LANES), BF16), jax.ShapeDtypeStruct((total // 2 + 8, total), F32)),
    )(spread, own, *arrived)

    summed = partial_gram + swap(partial_gram, "samp", 1)
    ready, summed = lax.optimization_barrier((centered, summed))
    across = swap(ready, "samp", 1)
    masks = [*range(2, lax.axis_size("par")), 1]
    summed = sum((swap(summed, "par", mask) for mask in masks), start=summed)
    parts = [summed, *swaps(summed, "samp", range(CORES, members, CORES)).values()]
    update, local_coeffs = kernel_call(
        functools.partial(solve_body, -math.sqrt(params_all / total)),
        (jax.ShapeDtypeStruct((CORES * mine, OFFSETS * LANES), F32), jax.ShapeDtypeStruct((1, samples), F32)),
    )(centered, across, *parts)
    update = in_order(update, "samp", range(CORES, members, CORES))
    return update, local_coeffs[0]


def local_gather(activations, cotangents, energies):
    samples, layers, channels, sites = activations.shape
    owned = cotangents.shape[2]
    position = lax.axis_index("samp")
    total = lax.axis_size("samp") * samples
    params_all = LAYERS * C * C * OFFSETS
    field = cotangents.reshape(samples, layers, owned, SIDE, SIDE)
    shifted = [jnp.roll(field, (row - 1, col - 1), axis=(3, 4)) for row in range(3) for col in range(3)]
    stacked = jnp.stack(shifted, axis=3).reshape(samples, layers, owned * OFFSETS, sites)
    grads = jnp.einsum("slkx,slix->slki", stacked, activations, preferred_element_type=F32)
    grads = grads.reshape(samples, layers, owned, OFFSETS, channels).transpose(0, 2, 1, 4, 3)
    grads = grads.reshape(samples, owned * layers * channels * OFFSETS)
    col_sums, energy_sum = lax.psum((jnp.sum(grads, axis=0), jnp.sum(energies)), "samp")
    centered = ((grads - col_sums / total) * (1.0 / math.sqrt(params_all))).astype(BF16)
    everyone = lax.all_gather(centered, "samp", axis=0, tiled=True)
    partial_gram = lax.dot_general(centered, everyone, (((1,), (1,)), ((), ())), preferred_element_type=F32)
    gram = lax.all_gather(lax.psum(partial_gram, "par"), "samp", axis=0, tiled=True)
    deviation = lax.all_gather(energies - energy_sum / total, "samp", axis=0, tiled=True)
    coeffs = solve_system(gram, deviation, total)
    local_coeffs = lax.dynamic_slice_in_dim(coeffs, position * samples, samples)
    term = jnp.dot(local_coeffs[None, :], centered.astype(F32), precision=lax.Precision.HIGHEST)[0]
    update = -math.sqrt(params_all / total) * lax.psum(term, "samp")
    return update.reshape(owned, -1), local_coeffs


def local(activations, cotangents, energies):
    if cotangents.shape[2] % lax.axis_size("samp"):
        return local_gather(activations, cotangents, energies)
    return local_split(activations, cotangents, energies)


def solution(mesh):
    return jax.shard_map(
        local,
        mesh=mesh,
        in_specs=(P("samp", None, None, None), P("samp", None, "par", None), P("samp")),
        out_specs=(P("par", None), P("samp")),
        check_vma=False,
    )
```

```python
import functools
import math

import jax
import jax.numpy as jnp
from jax import lax
from jax.experimental import pallas as pl
from jax.experimental.pallas import tpu as pltpu
from jax.sharding import PartitionSpec as P

C = 64
SIDE = 16
LAYERS = 2
SITES = SIDE * SIDE
OFFSETS = 9
LANES = 128
CORES = 2


reg_shift = 0.1
F32 = jnp.float32
BF16 = jnp.bfloat16
VMEM_LIMIT = 48 * 1024 * 1024


def kernel_call(body, out_shape, scratch_shapes=(), **options):
    return pl.pallas_call(
        body,
        out_shape=out_shape,
        **options,
        scratch_shapes=scratch_shapes,
        compiler_params=pltpu.CompilerParams(vmem_limit_bytes=VMEM_LIMIT),
    )


def swap(x, axis, mask):
    count = lax.axis_size(axis)
    return lax.ppermute(x, axis, [(i, i ^ mask) for i in range(count)])


def exponent(values):
    top = jnp.maximum(jnp.max(jnp.abs(values), axis=0, keepdims=True), 1e-30)
    return 14.0 - jnp.floor(jnp.log2(top))


def packed_rows(rows, samples):
    return -(-(rows * samples + rows + 2) // 8) * 8


def grads_body(far, acts_hbm, cots_hbm, *refs):
    *out_refs, acts_ref, cots_ref, shifted_ref, grads_ref, semaphores = refs
    copies = [
        pltpu.make_async_copy(cots_hbm, cots_ref, semaphores.at[0]),
        pltpu.make_async_copy(acts_hbm, acts_ref, semaphores.at[1]),
    ]
    for copy in copies:
        copy.start()
    samples, layers, owned, sites = cots_ref.shape
    members = len(out_refs)
    owned = owned // 2
    mine = owned // members
    rows = OFFSETS * mine
    moves = []
    source = lax.broadcasted_iota(jnp.int32, (sites, sites), 0)
    target = lax.broadcasted_iota(jnp.int32, (1, sites), 1)
    for offset in range(OFFSETS):
        row, col = target // SIDE, target % SIDE
        row = (row + SIDE - (offset // 3 - 1)) % SIDE
        col = (col + SIDE - (offset % 3 - 1)) % SIDE
        moves.append(jnp.where(source == row * SIDE + col, 1.0, 0.0).astype(BF16))
    position = lax.axis_index("samp")
    upper = (position // members + int(far)) % 2 == 1
    copies[0].wait()
    field = cots_ref[...].astype(F32).reshape(samples * layers, 2, owned, sites)
    field = jnp.where(upper, field[:, 1], field[:, 0]).reshape(samples * layers * owned, sites).astype(BF16)
    for offset in range(OFFSETS):
        shifted_ref[offset] = jnp.dot(field, moves[offset], preferred_element_type=F32).astype(BF16)
    copies[1].wait()
    lanes = grads_ref.shape[1]
    lane = lax.broadcasted_iota(jnp.int32, (OFFSETS, owned, lanes), 2)
    for sample in range(samples):
        first = sample * layers * owned
        left = jnp.concatenate([shifted_ref[k, first : first + layers * owned, :] for k in range(OFFSETS)], axis=0)
        right = acts_ref[sample].reshape(layers * C, sites)
        products = lax.dot_general(left, right, (((1,), (1,)), ((), ())), preferred_element_type=F32)
        products = products.reshape(OFFSETS, layers, owned, lanes)
        grads = products[:, 0]
        for layer in range(1, layers):
            grads = jnp.where(lane >= layer * C, products[:, layer], grads)
        grads_ref[pl.ds(sample, OFFSETS * owned, stride=samples), :] = grads.reshape(OFFSETS * owned, lanes)
    for index in range(members):
        slot = index + members * int(far)
        start = ((position ^ slot) % members) * (mine * samples)
        pieces = [
            grads_ref[pl.ds(pl.multiple_of(k * owned * samples + start, mine * samples), mine * samples), :] for k in range(OFFSETS)
        ]
        values = jnp.concatenate(pieces, axis=0).reshape(rows, samples, lanes)
        values_ref = out_refs[index]
        if slot == 0:
            values_ref[...] = values
            continue
        reference = (jnp.sum(values, axis=1) * (1.0 / samples)).astype(BF16).astype(F32)
        values = values - reference[:, None, :]
        shift = exponent(jnp.max(jnp.abs(values), axis=0))
        reference_shift = exponent(reference)
        last = rows * samples
        values_ref[0:last, :] = (values * jnp.exp2(shift)).reshape(last, lanes)
        values_ref[last : last + rows, :] = reference * jnp.exp2(reference_shift)
        values_ref[last + rows : last + rows + 1, :] = shift
        values_ref[last + rows + 1 : last + rows + 2, :] = reference_shift
        spare = values_ref.shape[0] - (last + rows + 2)
        if spare:
            values_ref[last + rows + 2 :, :] = jnp.zeros((spare, lanes), F32)


def halves(half):
    row = lax.broadcasted_iota(jnp.int32, (half, 2 * half), 0)
    lane = lax.broadcasted_iota(jnp.int32, (half, 2 * half), 1)
    return row, lane


def fold(matrix, energies):
    half = matrix.shape[0] // 2
    row, lane = halves(half)
    top, bottom = matrix[:half], matrix[half:]
    turned = pltpu.roll(bottom, half, 1)
    diagonal = jnp.sum(jnp.where(lane == row, turned, 0.0), axis=0, keepdims=True)
    first = lax.broadcasted_iota(jnp.int32, energies.shape, 0) == 0
    rest = jnp.where(first, diagonal, energies)
    return jnp.concatenate([jnp.where((lane > row) & (lane < half), turned, top), rest], axis=0)


def unfold(folded):
    half = folded.shape[1] // 2
    row, lane = halves(half)
    body, diagonal = folded[:half], folded[half : half + 1]
    flipped = body.T
    mixed, crossed = flipped[:half], flipped[half:]
    both = jnp.concatenate([mixed, crossed], axis=1)
    top = jnp.where((lane > row) & (lane < half), both, body)
    lower = jnp.concatenate([crossed, mixed], axis=1)
    turned = pltpu.roll(body, half, 1)
    place = lane - half
    corner = jnp.where(place > row, turned, jnp.where(place == row, pltpu.roll(jnp.broadcast_to(diagonal, turned.shape), half, 1), lower))
    return jnp.concatenate([top, jnp.where(lane < half, lower, corner)], axis=0)


def gram_body(total, params_all, energies_ref, own_ref, *refs):
    rows, group, lanes = own_ref.shape
    *value_refs, centered_ref, gram_ref = refs
    by_slot = dict(zip(far_first(len(value_refs) + 1), value_refs))
    value_refs = [by_slot[slot] for slot in sorted(by_slot)]
    position = lax.axis_index("samp")
    gram = jnp.zeros((total, total), F32)
    last = rows * group
    scales = [jnp.exp2(-ref[last + rows : last + rows + 1, :]) for ref in value_refs]
    references = [ref[last : last + rows, :] * jnp.exp2(-ref[last + rows + 1 : last + rows + 2, :]) for ref in value_refs]
    pair = []
    for row in range(rows):
        blocks = [own_ref[row]]
        for ref, scale, reference in zip(value_refs, scales, references):
            blocks.append(ref[row * group : (row + 1) * group, :] * scale + reference[row : row + 1, :])
        mean = sum(jnp.sum(block, axis=0, keepdims=True) for block in blocks) / total
        for slot in range(len(blocks)):
            place = pl.ds(pl.multiple_of((position ^ slot) * group, group), group)
            centered_ref[row, place, :] = ((blocks[slot] - mean) * (1.0 / math.sqrt(params_all))).astype(BF16)
        pair.append(centered_ref[row])
        if len(pair) == 2 or row == rows - 1:
            both = jnp.concatenate(pair, axis=1)
            gram = gram + lax.dot_general(both, both, (((1,), (1,)), ((), ())), preferred_element_type=F32)
            pair = []
    gram_ref[...] = fold(gram, energies_ref[...])


WIDTH = 16


def thirds(values):
    high = values.astype(BF16)
    rest = values - high.astype(F32)
    middle = rest.astype(BF16)
    return high, middle, (rest - middle.astype(F32)).astype(BF16)


def outer_sum(left, right):
    a, b, c = thirds(left)
    d, e, f = thirds(right)
    lefts = jnp.concatenate([a, a, b, a, b, c], axis=0)
    rights = jnp.concatenate([d, e, d, f, e, d], axis=0)
    return lax.dot_general(lefts, rights, (((0,), (0,)), ((), ())), preferred_element_type=F32)


def spread_lane(rows, lane):
    return jnp.broadcast_to(rows[:, lane : lane + 1], rows.shape)


def eliminate(block, panel, row):
    block = list(block)
    for step in range(0, len(block), 2):
        one, two = block[step], block[step + 1]
        a, b, c = one[step : step + 1], two[step : step + 1], two[step + 1 : step + 2]
        inverse = 1.0 / (a * c - b * b)
        upper_row, lower_row = row == step, row == step + 1
        done = upper_row | lower_row
        one = jnp.where(done, jnp.where(upper_row, -1.0, 0.0), one)
        two = jnp.where(done, jnp.where(lower_row, -1.0, 0.0), two)

        def reduced(rows):
            upper, lower = rows[step : step + 1], rows[step + 1 : step + 2]
            first, second = (c * upper - b * lower) * inverse, (a * lower - b * upper) * inverse
            return jnp.where(done, 0.0, rows) - (one * first + two * second)

        panel = reduced(panel)
        block = [reduced(rows) if c >= step + 2 else rows for c, rows in enumerate(block)]
    return panel


def invert(matrix):
    matrix = list(matrix)
    count, size = len(matrix), WIDTH * len(matrix)
    row = lax.broadcasted_iota(jnp.int32, (WIDTH, size), 0)
    lane = lax.broadcasted_iota(jnp.int32, (WIDTH, size), 1)
    pivot = matrix[0]
    for index in range(count):
        first = WIDTH * index
        inside = (lane >= first) & (lane < first + WIDTH)
        unit = jnp.where(lane == row + first, 1.0, 0.0)
        solved = eliminate([spread_lane(pivot, first + c) for c in range(WIDTH)], jnp.where(inside, unit, pivot), row)
        solved = jnp.where(inside, -solved, solved)
        update = outer_sum(jnp.where(inside, 0.0, pivot), solved)
        following = None
        if index + 1 < count:
            terms = [spread_lane(matrix[index + 1], first + c) * solved[c : c + 1] for c in range(WIDTH)]
            following = jnp.where(inside, 0.0, matrix[index + 1])
            for term in terms:
                following = following - term
        for other in range(count):
            if other == index:
                matrix[other] = solved
            elif other == index + 1:
                matrix[other] = following
            else:
                matrix[other] = jnp.where(inside, 0.0, matrix[other]) - update[WIDTH * other : WIDTH * (other + 1)]
        pivot = following
    return matrix


def arrange(terms):
    rows, lanes = len(terms), terms[0].shape[1]
    owned = rows // OFFSETS
    padded = -(-rows // 8) * 8
    table = jnp.concatenate(terms + [jnp.zeros((padded - rows, lanes), F32)], axis=0)
    row_index = lax.broadcasted_iota(jnp.int32, (padded, lanes), 0)
    tiles = []
    for tile in range(OFFSETS):
        place = lax.broadcasted_iota(jnp.int32, (padded, lanes), 1) + tile * lanes
        picked = jnp.take_along_axis(table, place // OFFSETS, axis=1)
        sums = []
        for channel in range(owned):
            mask = row_index == (place % OFFSETS) * owned + channel
            sums.append(jnp.sum(jnp.where(mask, picked, 0.0), axis=0, keepdims=True))
        tiles.append(jnp.concatenate(sums, axis=0))
    return jnp.concatenate(tiles, axis=1)


def solve_body(scale, centered_ref, across_ref, *refs):
    *part_refs, update_ref, coeffs_ref = refs
    rows, total, lanes = centered_ref.shape
    samples = coeffs_ref.shape[1]
    summed = part_refs[0][...]
    for ref in part_refs[1:]:
        summed = summed + ref[...]
    matrix = unfold(summed)
    row_index = lax.broadcasted_iota(jnp.int32, (WIDTH, total), 0)
    lane_index = lax.broadcasted_iota(jnp.int32, (WIDTH, total), 1)
    regular = [
        matrix[first : first + WIDTH] + jnp.where(lane_index == row_index + first, reg_shift, 0.0)
        for first in range(0, total, WIDTH)
    ]
    energies = summed[total // 2 + 1 : total // 2 + 2]
    deviation = energies - jnp.sum(energies, axis=1, keepdims=True) / total
    coeffs = jnp.concatenate([-jnp.sum(part * deviation, axis=1, keepdims=True) for part in invert(regular)], axis=0)

    position = lax.axis_index("samp")
    sample = lax.broadcasted_iota(jnp.int32, (total, lanes), 0)
    lane = lax.broadcasted_iota(jnp.int32, (total, lanes), 1)
    spread = jnp.broadcast_to(coeffs, (total, lanes))
    own = jnp.sum(jnp.where(sample == lane + position * samples, spread, 0.0), axis=0, keepdims=True)
    coeffs_ref[...] = own[:, :samples]

    spread = spread * scale
    own, across = (
        arrange([jnp.sum(ref[row].astype(F32) * spread, axis=0, keepdims=True) for row in range(rows)])
        for ref in (centered_ref, across_ref)
    )
    even = position % CORES == 0
    owned = own.shape[0]
    update_ref[0:owned, :] = jnp.where(even, own, across)
    update_ref[owned : 2 * owned, :] = jnp.where(even, across, own)


def far_first(members):
    return [*range(members // 2, members), *range(CORES, members // 2), *range(1, CORES)]


def swaps(x, axis, masks):
    return {mask: swap(x, axis, mask) for mask in sorted(masks, reverse=True)}


def in_order(x, axis, masks):
    blocks = {0: x, **swaps(x, axis, masks)}
    bits = lax.axis_index(axis) & functools.reduce(lambda a, b: a | b, masks)
    placed = []
    for place in sorted(blocks):
        block = blocks[0]
        for mask in sorted(masks):
            block = jnp.where(bits == place ^ mask, blocks[mask], block)
        placed.append(block)
    return jnp.concatenate(placed)


def solve_system(gram, dev_all, total):
    regular = gram + reg_shift * jnp.eye(total, dtype=F32)
    factor = jnp.linalg.cholesky(regular)
    forward = lax.linalg.triangular_solve(factor, dev_all[:, None], left_side=True, lower=True)
    return lax.linalg.triangular_solve(factor, forward, left_side=True, lower=True, transpose_a=True)[:, 0]


def local_split(activations, cotangents, energies):
    samples, layers, channels, sites = activations.shape
    owned = cotangents.shape[2]
    members = lax.axis_size("samp")
    chips = members // CORES
    total = members * samples
    position = lax.axis_index("samp")
    params_all = LAYERS * C * C * OFFSETS
    mine = owned // members
    rows = OFFSETS * mine

    own = jax.ShapeDtypeStruct((rows, samples, LANES), F32)
    block = jax.ShapeDtypeStruct((packed_rows(rows, samples), LANES), F32)
    inputs = [pltpu.with_memory_space_constraint(x, pltpu.HBM) for x in (activations, cotangents)]

    def half(far, out_shape):
        return kernel_call(
            functools.partial(grads_body, far),
            out_shape,
            [
                pltpu.VMEM(activations.shape, BF16),
                pltpu.VMEM(cotangents.shape, BF16),
                pltpu.VMEM((OFFSETS, samples * layers * owned // 2, sites), BF16),
                pltpu.VMEM(((OFFSETS * owned // 2 + 1) * samples, LANES), F32),
                pltpu.SemaphoreType.DMA((2,)),
            ],
            in_specs=[pl.BlockSpec(memory_space=pltpu.HBM)] * 2,
        )(*inputs)

    far_blocks = half(True, (block,) * (members // 2))
    own, *near_blocks = half(False, (own,) + (block,) * (members // 2 - 1))
    blocks = [*near_blocks, *far_blocks]
    order = far_first(members)
    arrived = [swap(blocks[slot - 1].astype(jnp.float16), "samp", slot).astype(F32) for slot in order]

    lane = jnp.arange(total) // samples
    here = (lane == position) & (lax.axis_index("par") == 0)
    spread = jnp.where(here, jnp.tile(energies, members), 0.0)
    spread = jnp.where(jnp.arange(8)[:, None] == 1, spread[None, :], 0.0)
    centered, partial_gram = kernel_call(
        functools.partial(gram_body, total, params_all),
        (jax.ShapeDtypeStruct((rows, total, LANES), BF16), jax.ShapeDtypeStruct((total // 2 + 8, total), F32)),
    )(spread, own, *arrived)

    summed = partial_gram + swap(partial_gram, "samp", 1)
    ready, summed = lax.optimization_barrier((centered, summed))
    across = swap(ready, "samp", 1)
    masks = [*range(2, lax.axis_size("par")), 1]
    summed = sum((swap(summed, "par", mask) for mask in masks), start=summed)
    parts = [summed, *swaps(summed, "samp", range(CORES, members, CORES)).values()]
    update, local_coeffs = kernel_call(
        functools.partial(solve_body, -math.sqrt(params_all / total)),
        (jax.ShapeDtypeStruct((CORES * mine, OFFSETS * LANES), F32), jax.ShapeDtypeStruct((1, samples), F32)),
    )(centered, across, *parts)
    update = in_order(update, "samp", range(CORES, members, CORES))
    return update, local_coeffs[0]


def local_gather(activations, cotangents, energies):
    samples, layers, channels, sites = activations.shape
    owned = cotangents.shape[2]
    position = lax.axis_index("samp")
    total = lax.axis_size("samp") * samples
    params_all = LAYERS * C * C * OFFSETS
    field = cotangents.reshape(samples, layers, owned, SIDE, SIDE)
    shifted = [jnp.roll(field, (row - 1, col - 1), axis=(3, 4)) for row in range(3) for col in range(3)]
    stacked = jnp.stack(shifted, axis=3).reshape(samples, layers, owned * OFFSETS, sites)
    grads = jnp.einsum("slkx,slix->slki", stacked, activations, preferred_element_type=F32)
    grads = grads.reshape(samples, layers, owned, OFFSETS, channels).transpose(0, 2, 1, 4, 3)
    grads = grads.reshape(samples, owned * layers * channels * OFFSETS)
    col_sums, energy_sum = lax.psum((jnp.sum(grads, axis=0), jnp.sum(energies)), "samp")
    centered = ((grads - col_sums / total) * (1.0 / math.sqrt(params_all))).astype(BF16)
    everyone = lax.all_gather(centered, "samp", axis=0, tiled=True)
    partial_gram = lax.dot_general(centered, everyone, (((1,), (1,)), ((), ())), preferred_element_type=F32)
    gram = lax.all_gather(lax.psum(partial_gram, "par"), "samp", axis=0, tiled=True)
    deviation = lax.all_gather(energies - energy_sum / total, "samp", axis=0, tiled=True)
    coeffs = solve_system(gram, deviation, total)
    local_coeffs = lax.dynamic_slice_in_dim(coeffs, position * samples, samples)
    term = jnp.dot(local_coeffs[None, :], centered.astype(F32), precision=lax.Precision.HIGHEST)[0]
    update = -math.sqrt(params_all / total) * lax.psum(term, "samp")
    return update.reshape(owned, -1), local_coeffs


def local(activations, cotangents, energies):
    if cotangents.shape[2] % lax.axis_size("samp"):
        return local_gather(activations, cotangents, energies)
    return local_split(activations, cotangents, energies)


def solution(mesh):
    return jax.shard_map(
        local,
        mesh=mesh,
        in_specs=(P("samp", None, None, None), P("samp", None, "par", None), P("samp")),
        out_specs=(P("par", None), P("samp")),
        check_vma=False,
    )
```

```python
import functools
import math

import jax
import jax.numpy as jnp
from jax import lax
from jax.experimental import pallas as pl
from jax.experimental.pallas import tpu as pltpu
from jax.sharding import PartitionSpec as P

C = 64
SIDE = 16
LAYERS = 2
SITES = SIDE * SIDE
OFFSETS = 9
LANES = 128
CORES = 2


reg_shift = 0.1
F32 = jnp.float32
BF16 = jnp.bfloat16
VMEM_LIMIT = 48 * 1024 * 1024


def kernel_call(body, out_shape, scratch_shapes=(), **options):
    return pl.pallas_call(
        body,
        out_shape=out_shape,
        **options,
        scratch_shapes=scratch_shapes,
        compiler_params=pltpu.CompilerParams(vmem_limit_bytes=VMEM_LIMIT),
    )


def swap(x, axis, mask):
    count = lax.axis_size(axis)
    return lax.ppermute(x, axis, [(i, i ^ mask) for i in range(count)])


def exponent(values):
    top = jnp.maximum(jnp.max(jnp.abs(values), axis=0, keepdims=True), 1e-30)
    return 14.0 - jnp.floor(jnp.log2(top))


def packed_rows(rows, samples):
    return -(-(rows * samples + rows + 2) // 8) * 8


def grads_body(far, acts_hbm, cots_hbm, *refs):
    *out_refs, acts_ref, cots_ref, shifted_ref, grads_ref, semaphores = refs
    copies = [
        pltpu.make_async_copy(cots_hbm, cots_ref, semaphores.at[0]),
        pltpu.make_async_copy(acts_hbm, acts_ref, semaphores.at[1]),
    ]
    for copy in copies:
        copy.start()
    samples, layers, owned, sites = cots_ref.shape
    members = len(out_refs)
    owned = owned // 2
    mine = owned // members
    rows = OFFSETS * mine
    moves = []
    source = lax.broadcasted_iota(jnp.int32, (sites, sites), 0)
    target = lax.broadcasted_iota(jnp.int32, (1, sites), 1)
    for offset in range(OFFSETS):
        row, col = target // SIDE, target % SIDE
        row = (row + SIDE - (offset // 3 - 1)) % SIDE
        col = (col + SIDE - (offset % 3 - 1)) % SIDE
        moves.append(jnp.where(source == row * SIDE + col, 1.0, 0.0).astype(BF16))
    position = lax.axis_index("samp")
    upper = (position // members + int(far)) % 2 == 1
    copies[0].wait()
    field = cots_ref[...].astype(F32).reshape(samples * layers, 2, owned, sites)
    field = jnp.where(upper, field[:, 1], field[:, 0]).reshape(samples * layers * owned, sites).astype(BF16)
    for offset in range(OFFSETS):
        shifted_ref[offset] = jnp.dot(field, moves[offset], preferred_element_type=F32).astype(BF16)
    copies[1].wait()
    lanes = grads_ref.shape[1]
    lane = lax.broadcasted_iota(jnp.int32, (OFFSETS, owned, lanes), 2)
    for sample in range(samples):
        first = sample * layers * owned
        left = jnp.concatenate([shifted_ref[k, first : first + layers * owned, :] for k in range(OFFSETS)], axis=0)
        right = acts_ref[sample].reshape(layers * C, sites)
        products = lax.dot_general(left, right, (((1,), (1,)), ((), ())), preferred_element_type=F32)
        products = products.reshape(OFFSETS, layers, owned, lanes)
        grads = products[:, 0]
        for layer in range(1, layers):
            grads = jnp.where(lane >= layer * C, products[:, layer], grads)
        grads_ref[pl.ds(sample, OFFSETS * owned, stride=samples), :] = grads.reshape(OFFSETS * owned, lanes)
    for index in range(members):
        slot = index + members * int(far)
        start = ((position ^ slot) % members) * (mine * samples)
        pieces = [
            grads_ref[pl.ds(pl.multiple_of(k * owned * samples + start, mine * samples), mine * samples), :] for k in range(OFFSETS)
        ]
        values = jnp.concatenate(pieces, axis=0).reshape(rows, samples, lanes)
        values_ref = out_refs[index]
        if slot == 0:
            values_ref[...] = values
            continue
        reference = (jnp.sum(values, axis=1) * (1.0 / samples)).astype(BF16).astype(F32)
        values = values - reference[:, None, :]
        shift = exponent(jnp.max(jnp.abs(values), axis=0))
        reference_shift = exponent(reference)
        last = rows * samples
        values_ref[0:last, :] = (values * jnp.exp2(shift)).reshape(last, lanes)
        values_ref[last : last + rows, :] = reference * jnp.exp2(reference_shift)
        values_ref[last + rows : last + rows + 1, :] = shift
        values_ref[last + rows + 1 : last + rows + 2, :] = reference_shift
        spare = values_ref.shape[0] - (last + rows + 2)
        if spare:
            values_ref[last + rows + 2 :, :] = jnp.zeros((spare, lanes), F32)


def halves(half):
    row = lax.broadcasted_iota(jnp.int32, (half, 2 * half), 0)
    lane = lax.broadcasted_iota(jnp.int32, (half, 2 * half), 1)
    return row, lane


def fold(matrix, energies):
    half = matrix.shape[0] // 2
    row, lane = halves(half)
    top, bottom = matrix[:half], matrix[half:]
    turned = pltpu.roll(bottom, half, 1)
    diagonal = jnp.sum(jnp.where(lane == row, turned, 0.0), axis=0, keepdims=True)
    first = lax.broadcasted_iota(jnp.int32, energies.shape, 0) == 0
    rest = jnp.where(first, diagonal, energies)
    return jnp.concatenate([jnp.where((lane > row) & (lane < half), turned, top), rest], axis=0)


def unfold(folded):
    half = folded.shape[1] // 2
    row, lane = halves(half)
    body, diagonal = folded[:half], folded[half : half + 1]
    flipped = body.T
    mixed, crossed = flipped[:half], flipped[half:]
    both = jnp.concatenate([mixed, crossed], axis=1)
    top = jnp.where((lane > row) & (lane < half), both, body)
    lower = jnp.concatenate([crossed, mixed], axis=1)
    turned = pltpu.roll(body, half, 1)
    place = lane - half
    corner = jnp.where(place > row, turned, jnp.where(place == row, pltpu.roll(jnp.broadcast_to(diagonal, turned.shape), half, 1), lower))
    return jnp.concatenate([top, jnp.where(lane < half, lower, corner)], axis=0)


def gram_body(total, params_all, energies_ref, own_ref, *refs):
    rows, group, lanes = own_ref.shape
    *value_refs, centered_ref, gram_ref = refs
    by_slot = dict(zip(far_first(len(value_refs) + 1), value_refs))
    value_refs = [by_slot[slot] for slot in sorted(by_slot)]
    position = lax.axis_index("samp")
    gram = jnp.zeros((total, total), F32)
    last = rows * group
    scales = [jnp.exp2(-ref[last + rows : last + rows + 1, :]) for ref in value_refs]
    references = [ref[last : last + rows, :] * jnp.exp2(-ref[last + rows + 1 : last + rows + 2, :]) for ref in value_refs]
    pair = []
    for row in range(rows):
        blocks = [own_ref[row]]
        for ref, scale, reference in zip(value_refs, scales, references):
            blocks.append(ref[row * group : (row + 1) * group, :] * scale + reference[row : row + 1, :])
        mean = sum(jnp.sum(block, axis=0, keepdims=True) for block in blocks) / total
        for slot in range(len(blocks)):
            place = pl.ds(pl.multiple_of((position ^ slot) * group, group), group)
            centered_ref[row, place, :] = ((blocks[slot] - mean) * (1.0 / math.sqrt(params_all))).astype(BF16)
        pair.append(centered_ref[row])
        if len(pair) == 2 or row == rows - 1:
            both = jnp.concatenate(pair, axis=1)
            gram = gram + lax.dot_general(both, both, (((1,), (1,)), ((), ())), preferred_element_type=F32)
            pair = []
    gram_ref[...] = fold(gram, energies_ref[...])


WIDTH = 16


def thirds(values):
    high = values.astype(BF16)
    rest = values - high.astype(F32)
    middle = rest.astype(BF16)
    return high, middle, (rest - middle.astype(F32)).astype(BF16)


def outer_sum(left, right):
    a, b, c = thirds(left)
    d, e, f = thirds(right)
    lefts = jnp.concatenate([a, a, b, a, b, c], axis=0)
    rights = jnp.concatenate([d, e, d, f, e, d], axis=0)
    return lax.dot_general(lefts, rights, (((0,), (0,)), ((), ())), preferred_element_type=F32)


def spread_lane(rows, lane):
    return jnp.broadcast_to(rows[:, lane : lane + 1], rows.shape)


def eliminate(block, panel, row):
    block = list(block)
    for step in range(0, len(block), 2):
        one, two = block[step], block[step + 1]
        a, b, c = one[step : step + 1], two[step : step + 1], two[step + 1 : step + 2]
        inverse = 1.0 / (a * c - b * b)
        upper_row, lower_row = row == step, row == step + 1
        done = upper_row | lower_row
        one = jnp.where(done, jnp.where(upper_row, -1.0, 0.0), one)
        two = jnp.where(done, jnp.where(lower_row, -1.0, 0.0), two)

        def reduced(rows):
            upper, lower = rows[step : step + 1], rows[step + 1 : step + 2]
            first, second = (c * upper - b * lower) * inverse, (a * lower - b * upper) * inverse
            return jnp.where(done, 0.0, rows) - (one * first + two * second)

        panel = reduced(panel)
        block = [reduced(rows) if c >= step + 2 else rows for c, rows in enumerate(block)]
    return panel


def as_column(values, rows, first):
    row = lax.broadcasted_iota(jnp.int32, (rows, values.shape[1]), 0)
    lane = lax.broadcasted_iota(jnp.int32, (rows, values.shape[1]), 1)
    return jnp.sum(jnp.where(lane == row + first, values, 0.0), axis=1, keepdims=True)


def solve_symmetric(matrix, right):
    matrix = list(matrix)
    count, size = len(matrix), WIDTH * len(matrix)
    row = lax.broadcasted_iota(jnp.int32, (WIDTH, size), 0)
    lane = lax.broadcasted_iota(jnp.int32, (WIDTH, size), 1)
    columns = [as_column(right, WIDTH, WIDTH * index) for index in range(count)]
    pivot = matrix[0]
    for index in range(count):
        first = WIDTH * index
        inside = (lane >= first) & (lane < first + WIDTH)
        unit = jnp.where(lane == row + first, 1.0, 0.0)
        solved = eliminate([spread_lane(pivot, first + c) for c in range(WIDTH)], jnp.where(inside, unit, pivot), row)
        solved = jnp.where(inside, -solved, solved)
        held = jnp.where(inside, 0.0, pivot)
        if index + 1 == count:
            weights = columns[index] - jnp.sum(held * right, axis=1, keepdims=True)
            terms = [jnp.where(inside, 0.0, matrix[other]) * columns[other] for other in range(index)]
            return -jnp.sum(sum(terms) + solved * weights, axis=0, keepdims=True)
        update = outer_sum(held, solved)
        following = jnp.where(inside, 0.0, matrix[index + 1])
        for c in range(WIDTH):
            following = following - spread_lane(matrix[index + 1], first + c) * solved[c : c + 1]
        for other in range(count):
            if other == index:
                matrix[other] = solved
            elif other == index + 1:
                matrix[other] = following
            else:
                matrix[other] = jnp.where(inside, 0.0, matrix[other]) - update[WIDTH * other : WIDTH * (other + 1)]
        pivot = following


def arrange(terms):
    rows, lanes = len(terms), terms[0].shape[1]
    owned = rows // OFFSETS
    padded = -(-rows // 8) * 8
    table = jnp.concatenate(terms + [jnp.zeros((padded - rows, lanes), F32)], axis=0)
    row_index = lax.broadcasted_iota(jnp.int32, (padded, lanes), 0)
    tiles = []
    for tile in range(OFFSETS):
        place = lax.broadcasted_iota(jnp.int32, (padded, lanes), 1) + tile * lanes
        picked = jnp.take_along_axis(table, place // OFFSETS, axis=1)
        sums = []
        for channel in range(owned):
            mask = row_index == (place % OFFSETS) * owned + channel
            sums.append(jnp.sum(jnp.where(mask, picked, 0.0), axis=0, keepdims=True))
        tiles.append(jnp.concatenate(sums, axis=0))
    return jnp.concatenate(tiles, axis=1)


def solve_body(scale, centered_ref, across_ref, *refs):
    *part_refs, update_ref, coeffs_ref = refs
    rows, total, lanes = centered_ref.shape
    samples = coeffs_ref.shape[1]
    summed = part_refs[0][...]
    for ref in part_refs[1:]:
        summed = summed + ref[...]
    matrix = unfold(summed)
    row_index = lax.broadcasted_iota(jnp.int32, (WIDTH, total), 0)
    lane_index = lax.broadcasted_iota(jnp.int32, (WIDTH, total), 1)
    regular = [
        matrix[first : first + WIDTH] + jnp.where(lane_index == row_index + first, reg_shift, 0.0)
        for first in range(0, total, WIDTH)
    ]
    energies = summed[total // 2 + 1 : total // 2 + 2]
    deviation = energies - jnp.sum(energies, axis=1, keepdims=True) / total
    coeffs = as_column(solve_symmetric(regular, deviation), total, 0)

    position = lax.axis_index("samp")
    sample = lax.broadcasted_iota(jnp.int32, (total, lanes), 0)
    lane = lax.broadcasted_iota(jnp.int32, (total, lanes), 1)
    spread = jnp.broadcast_to(coeffs, (total, lanes))
    own = jnp.sum(jnp.where(sample == lane + position * samples, spread, 0.0), axis=0, keepdims=True)
    coeffs_ref[...] = own[:, :samples]

    spread = spread * scale
    own, across = (
        arrange([jnp.sum(ref[row].astype(F32) * spread, axis=0, keepdims=True) for row in range(rows)])
        for ref in (centered_ref, across_ref)
    )
    even = position % CORES == 0
    owned = own.shape[0]
    update_ref[0:owned, :] = jnp.where(even, own, across)
    update_ref[owned : 2 * owned, :] = jnp.where(even, across, own)


def far_first(members):
    return [*range(members // 2, members), *range(CORES, members // 2), *range(1, CORES)]


def swaps(x, axis, masks):
    return {mask: swap(x, axis, mask) for mask in sorted(masks, reverse=True)}


def in_order(x, axis, masks):
    blocks = {0: x, **swaps(x, axis, masks)}
    bits = lax.axis_index(axis) & functools.reduce(lambda a, b: a | b, masks)
    placed = []
    for place in sorted(blocks):
        block = blocks[0]
        for mask in sorted(masks):
            block = jnp.where(bits == place ^ mask, blocks[mask], block)
        placed.append(block)
    return jnp.concatenate(placed)


def solve_system(gram, dev_all, total):
    regular = gram + reg_shift * jnp.eye(total, dtype=F32)
    factor = jnp.linalg.cholesky(regular)
    forward = lax.linalg.triangular_solve(factor, dev_all[:, None], left_side=True, lower=True)
    return lax.linalg.triangular_solve(factor, forward, left_side=True, lower=True, transpose_a=True)[:, 0]


def local_split(activations, cotangents, energies):
    samples, layers, channels, sites = activations.shape
    owned = cotangents.shape[2]
    members = lax.axis_size("samp")
    chips = members // CORES
    total = members * samples
    position = lax.axis_index("samp")
    params_all = LAYERS * C * C * OFFSETS
    mine = owned // members
    rows = OFFSETS * mine

    own = jax.ShapeDtypeStruct((rows, samples, LANES), F32)
    block = jax.ShapeDtypeStruct((packed_rows(rows, samples), LANES), F32)
    inputs = [pltpu.with_memory_space_constraint(x, pltpu.HBM) for x in (activations, cotangents)]

    def half(far, out_shape):
        return kernel_call(
            functools.partial(grads_body, far),
            out_shape,
            [
                pltpu.VMEM(activations.shape, BF16),
                pltpu.VMEM(cotangents.shape, BF16),
                pltpu.VMEM((OFFSETS, samples * layers * owned // 2, sites), BF16),
                pltpu.VMEM(((OFFSETS * owned // 2 + 1) * samples, LANES), F32),
                pltpu.SemaphoreType.DMA((2,)),
            ],
            in_specs=[pl.BlockSpec(memory_space=pltpu.HBM)] * 2,
        )(*inputs)

    far_blocks = half(True, (block,) * (members // 2))
    own, *near_blocks = half(False, (own,) + (block,) * (members // 2 - 1))
    blocks = [*near_blocks, *far_blocks]
    order = far_first(members)
    arrived = [swap(blocks[slot - 1].astype(jnp.float16), "samp", slot).astype(F32) for slot in order]

    lane = jnp.arange(total) // samples
    here = (lane == position) & (lax.axis_index("par") == 0)
    spread = jnp.where(here, jnp.tile(energies, members), 0.0)
    spread = jnp.where(jnp.arange(8)[:, None] == 1, spread[None, :], 0.0)
    centered, partial_gram = kernel_call(
        functools.partial(gram_body, total, params_all),
        (jax.ShapeDtypeStruct((rows, total, LANES), BF16), jax.ShapeDtypeStruct((total // 2 + 8, total), F32)),
    )(spread, own, *arrived)

    summed = partial_gram + swap(partial_gram, "samp", 1)
    ready, summed = lax.optimization_barrier((centered, summed))
    across = swap(ready, "samp", 1)
    masks = [*range(2, lax.axis_size("par")), 1]
    summed = sum((swap(summed, "par", mask) for mask in masks), start=summed)
    parts = [summed, *swaps(summed, "samp", range(CORES, members, CORES)).values()]
    update, local_coeffs = kernel_call(
        functools.partial(solve_body, -math.sqrt(params_all / total)),
        (jax.ShapeDtypeStruct((CORES * mine, OFFSETS * LANES), F32), jax.ShapeDtypeStruct((1, samples), F32)),
    )(centered, across, *parts)
    update = in_order(update, "samp", range(CORES, members, CORES))
    return update, local_coeffs[0]


def local_gather(activations, cotangents, energies):
    samples, layers, channels, sites = activations.shape
    owned = cotangents.shape[2]
    position = lax.axis_index("samp")
    total = lax.axis_size("samp") * samples
    params_all = LAYERS * C * C * OFFSETS
    field = cotangents.reshape(samples, layers, owned, SIDE, SIDE)
    shifted = [jnp.roll(field, (row - 1, col - 1), axis=(3, 4)) for row in range(3) for col in range(3)]
    stacked = jnp.stack(shifted, axis=3).reshape(samples, layers, owned * OFFSETS, sites)
    grads = jnp.einsum("slkx,slix->slki", stacked, activations, preferred_element_type=F32)
    grads = grads.reshape(samples, layers, owned, OFFSETS, channels).transpose(0, 2, 1, 4, 3)
    grads = grads.reshape(samples, owned * layers * channels * OFFSETS)
    col_sums, energy_sum = lax.psum((jnp.sum(grads, axis=0), jnp.sum(energies)), "samp")
    centered = ((grads - col_sums / total) * (1.0 / math.sqrt(params_all))).astype(BF16)
    everyone = lax.all_gather(centered, "samp", axis=0, tiled=True)
    partial_gram = lax.dot_general(centered, everyone, (((1,), (1,)), ((), ())), preferred_element_type=F32)
    gram = lax.all_gather(lax.psum(partial_gram, "par"), "samp", axis=0, tiled=True)
    deviation = lax.all_gather(energies - energy_sum / total, "samp", axis=0, tiled=True)
    coeffs = solve_system(gram, deviation, total)
    local_coeffs = lax.dynamic_slice_in_dim(coeffs, position * samples, samples)
    term = jnp.dot(local_coeffs[None, :], centered.astype(F32), precision=lax.Precision.HIGHEST)[0]
    update = -math.sqrt(params_all / total) * lax.psum(term, "samp")
    return update.reshape(owned, -1), local_coeffs


def local(activations, cotangents, energies):
    if cotangents.shape[2] % lax.axis_size("samp"):
        return local_gather(activations, cotangents, energies)
    return local_split(activations, cotangents, energies)


def solution(mesh):
    return jax.shard_map(
        local,
        mesh=mesh,
        in_specs=(P("samp", None, None, None), P("samp", None, "par", None), P("samp")),
        out_specs=(P("par", None), P("samp")),
        check_vma=False,
    )
```

```python
import functools
import math

import jax
import jax.numpy as jnp
from jax import lax
from jax.experimental import pallas as pl
from jax.experimental.pallas import tpu as pltpu
from jax.sharding import PartitionSpec as P

C = 64
SIDE = 16
LAYERS = 2
SITES = SIDE * SIDE
OFFSETS = 9
LANES = 128
CORES = 2


reg_shift = 0.1
F32 = jnp.float32
BF16 = jnp.bfloat16
VMEM_LIMIT = 48 * 1024 * 1024


def kernel_call(body, out_shape, scratch_shapes=(), **options):
    return pl.pallas_call(
        body,
        out_shape=out_shape,
        **options,
        scratch_shapes=scratch_shapes,
        compiler_params=pltpu.CompilerParams(vmem_limit_bytes=VMEM_LIMIT),
    )


def swap(x, axis, mask):
    count = lax.axis_size(axis)
    return lax.ppermute(x, axis, [(i, i ^ mask) for i in range(count)])


def exponent(values):
    top = jnp.maximum(jnp.max(jnp.abs(values), axis=0, keepdims=True), 1e-30)
    return 14.0 - jnp.floor(jnp.log2(top))


def packed_rows(rows, samples):
    return -(-(rows * samples + rows + 2) // 8) * 8


def grads_body(far, acts_hbm, cots_hbm, *refs):
    *out_refs, acts_ref, cots_ref, shifted_ref, grads_ref, semaphores = refs
    copies = [
        pltpu.make_async_copy(cots_hbm, cots_ref, semaphores.at[0]),
        pltpu.make_async_copy(acts_hbm, acts_ref, semaphores.at[1]),
    ]
    for copy in copies:
        copy.start()
    samples, layers, owned, sites = cots_ref.shape
    members = len(out_refs)
    owned = owned // 2
    mine = owned // members
    rows = OFFSETS * mine
    moves = []
    source = lax.broadcasted_iota(jnp.int32, (sites, sites), 0)
    target = lax.broadcasted_iota(jnp.int32, (1, sites), 1)
    for offset in range(OFFSETS):
        row, col = target // SIDE, target % SIDE
        row = (row + SIDE - (offset // 3 - 1)) % SIDE
        col = (col + SIDE - (offset % 3 - 1)) % SIDE
        moves.append(jnp.where(source == row * SIDE + col, 1.0, 0.0).astype(BF16))
    position = lax.axis_index("samp")
    upper = (position // members + int(far)) % 2 == 1
    copies[0].wait()
    field = cots_ref[...].astype(F32).reshape(samples * layers, 2, owned, sites)
    field = jnp.where(upper, field[:, 1], field[:, 0]).reshape(samples * layers * owned, sites).astype(BF16)
    for offset in range(OFFSETS):
        shifted_ref[offset] = jnp.dot(field, moves[offset], preferred_element_type=F32).astype(BF16)
    copies[1].wait()
    lanes = grads_ref.shape[1]
    lane = lax.broadcasted_iota(jnp.int32, (OFFSETS, owned, lanes), 2)
    for sample in range(samples):
        first = sample * layers * owned
        left = jnp.concatenate([shifted_ref[k, first : first + layers * owned, :] for k in range(OFFSETS)], axis=0)
        right = acts_ref[sample].reshape(layers * C, sites)
        products = lax.dot_general(left, right, (((1,), (1,)), ((), ())), preferred_element_type=F32)
        products = products.reshape(OFFSETS, layers, owned, lanes)
        grads = products[:, 0]
        for layer in range(1, layers):
            grads = jnp.where(lane >= layer * C, products[:, layer], grads)
        grads_ref[pl.ds(sample, OFFSETS * owned, stride=samples), :] = grads.reshape(OFFSETS * owned, lanes)
    for index in range(members):
        slot = index + members * int(far)
        start = ((position ^ slot) % members) * (mine * samples)
        pieces = [
            grads_ref[pl.ds(pl.multiple_of(k * owned * samples + start, mine * samples), mine * samples), :] for k in range(OFFSETS)
        ]
        values = jnp.concatenate(pieces, axis=0).reshape(rows, samples, lanes)
        values_ref = out_refs[index]
        if slot == 0:
            values_ref[...] = values
            continue
        reference = (jnp.sum(values, axis=1) * (1.0 / samples)).astype(BF16).astype(F32)
        values = values - reference[:, None, :]
        shift = exponent(jnp.max(jnp.abs(values), axis=0))
        reference_shift = exponent(reference)
        last = rows * samples
        values_ref[0:last, :] = (values * jnp.exp2(shift)).reshape(last, lanes)
        values_ref[last : last + rows, :] = reference * jnp.exp2(reference_shift)
        values_ref[last + rows : last + rows + 1, :] = shift
        values_ref[last + rows + 1 : last + rows + 2, :] = reference_shift
        spare = values_ref.shape[0] - (last + rows + 2)
        if spare:
            values_ref[last + rows + 2 :, :] = jnp.zeros((spare, lanes), F32)


def halves(half):
    row = lax.broadcasted_iota(jnp.int32, (half, 2 * half), 0)
    lane = lax.broadcasted_iota(jnp.int32, (half, 2 * half), 1)
    return row, lane


def fold(matrix, energies):
    half = matrix.shape[0] // 2
    row, lane = halves(half)
    top, bottom = matrix[:half], matrix[half:]
    turned = pltpu.roll(bottom, half, 1)
    diagonal = jnp.sum(jnp.where(lane == row, turned, 0.0), axis=0, keepdims=True)
    first = lax.broadcasted_iota(jnp.int32, energies.shape, 0) == 0
    rest = jnp.where(first, diagonal, energies)
    return jnp.concatenate([jnp.where((lane > row) & (lane < half), turned, top), rest], axis=0)


def unfold(folded):
    half = folded.shape[1] // 2
    row, lane = halves(half)
    body, diagonal = folded[:half], folded[half : half + 1]
    flipped = body.T
    mixed, crossed = flipped[:half], flipped[half:]
    both = jnp.concatenate([mixed, crossed], axis=1)
    top = jnp.where((lane > row) & (lane < half), both, body)
    lower = jnp.concatenate([crossed, mixed], axis=1)
    turned = pltpu.roll(body, half, 1)
    place = lane - half
    corner = jnp.where(place > row, turned, jnp.where(place == row, pltpu.roll(jnp.broadcast_to(diagonal, turned.shape), half, 1), lower))
    return jnp.concatenate([top, jnp.where(lane < half, lower, corner)], axis=0)


def gram_body(total, params_all, energies_ref, own_ref, *refs):
    rows, group, lanes = own_ref.shape
    *value_refs, centered_ref, gram_ref = refs
    by_slot = dict(zip(far_first(len(value_refs) + 1), value_refs))
    value_refs = [by_slot[slot] for slot in sorted(by_slot)]
    position = lax.axis_index("samp")
    gram = jnp.zeros((total, total), F32)
    last = rows * group
    scales = [jnp.exp2(-ref[last + rows : last + rows + 1, :]) for ref in value_refs]
    references = [ref[last : last + rows, :] * jnp.exp2(-ref[last + rows + 1 : last + rows + 2, :]) for ref in value_refs]
    pair = []
    for row in range(rows):
        blocks = [own_ref[row]]
        for ref, scale, reference in zip(value_refs, scales, references):
            blocks.append(ref[row * group : (row + 1) * group, :] * scale + reference[row : row + 1, :])
        mean = sum(jnp.sum(block, axis=0, keepdims=True) for block in blocks) / total
        for slot in range(len(blocks)):
            place = pl.ds(pl.multiple_of((position ^ slot) * group, group), group)
            centered_ref[row, place, :] = ((blocks[slot] - mean) * (1.0 / math.sqrt(params_all))).astype(BF16)
        pair.append(centered_ref[row])
        if len(pair) == 2 or row == rows - 1:
            both = jnp.concatenate(pair, axis=1)
            gram = gram + lax.dot_general(both, both, (((1,), (1,)), ((), ())), preferred_element_type=F32)
            pair = []
    gram_ref[...] = fold(gram, energies_ref[...])


WIDTH = 16


def thirds(values):
    high = values.astype(BF16)
    rest = values - high.astype(F32)
    middle = rest.astype(BF16)
    return high, middle, (rest - middle.astype(F32)).astype(BF16)


def outer_sum(left, right):
    a, b, c = thirds(left)
    d, e, f = thirds(right)
    lefts = jnp.concatenate([a, a, b, a, b, c], axis=0)
    rights = jnp.concatenate([d, e, d, f, e, d], axis=0)
    return lax.dot_general(lefts, rights, (((0,), (0,)), ((), ())), preferred_element_type=F32)


def spread_lane(rows, lane):
    return jnp.broadcast_to(rows[:, lane : lane + 1], rows.shape)


def eliminate(block, panel, row):
    block = list(block)
    for step in range(0, len(block), 2):
        one, two = block[step], block[step + 1]
        a, b, c = one[step : step + 1], two[step : step + 1], two[step + 1 : step + 2]
        inverse = 1.0 / (a * c - b * b)
        upper_row, lower_row = row == step, row == step + 1
        done = upper_row | lower_row
        one = jnp.where(done, jnp.where(upper_row, -1.0, 0.0), one)
        two = jnp.where(done, jnp.where(lower_row, -1.0, 0.0), two)

        def reduced(rows):
            upper, lower = rows[step : step + 1], rows[step + 1 : step + 2]
            first, second = (c * upper - b * lower) * inverse, (a * lower - b * upper) * inverse
            return jnp.where(done, 0.0, rows) - (one * first + two * second)

        panel = reduced(panel)
        block = [reduced(rows) if c >= step + 2 else rows for c, rows in enumerate(block)]
    return panel


def as_column(values, rows, first):
    row = lax.broadcasted_iota(jnp.int32, (rows, values.shape[1]), 0)
    lane = lax.broadcasted_iota(jnp.int32, (rows, values.shape[1]), 1)
    return jnp.sum(jnp.where(lane == row + first, values, 0.0), axis=1, keepdims=True)


def solve_symmetric(matrix, right):
    matrix = list(matrix)
    count, size = len(matrix), WIDTH * len(matrix)
    row = lax.broadcasted_iota(jnp.int32, (WIDTH, size), 0)
    lane = lax.broadcasted_iota(jnp.int32, (WIDTH, size), 1)
    columns = [as_column(right, WIDTH, WIDTH * index) for index in range(count)]
    pivot = matrix[0]
    for index in range(count):
        first = WIDTH * index
        inside = (lane >= first) & (lane < first + WIDTH)
        unit = jnp.where(lane == row + first, 1.0, 0.0)
        solved = eliminate([spread_lane(pivot, first + c) for c in range(WIDTH)], jnp.where(inside, unit, pivot), row)
        solved = jnp.where(inside, -solved, solved)
        held = jnp.where(inside, 0.0, pivot)
        if index + 1 == count:
            weights = columns[index] - jnp.sum(held * right, axis=1, keepdims=True)
            terms = [jnp.where(inside, 0.0, matrix[other]) * columns[other] for other in range(index)]
            return -jnp.sum(sum(terms) + solved * weights, axis=0, keepdims=True)
        update = outer_sum(held, solved)
        following = jnp.where(inside, 0.0, matrix[index + 1])
        for c in range(WIDTH):
            following = following - spread_lane(matrix[index + 1], first + c) * solved[c : c + 1]
        for other in range(count):
            if other == index:
                matrix[other] = solved
            elif other == index + 1:
                matrix[other] = following
            else:
                matrix[other] = jnp.where(inside, 0.0, matrix[other]) - update[WIDTH * other : WIDTH * (other + 1)]
        pivot = following


def arrange(terms):
    rows, lanes = len(terms), terms[0].shape[1]
    owned = rows // OFFSETS
    padded = -(-rows // 8) * 8
    table = jnp.concatenate(terms + [jnp.zeros((padded - rows, lanes), F32)], axis=0)
    row_index = lax.broadcasted_iota(jnp.int32, (padded, lanes), 0)
    tiles = []
    for tile in range(OFFSETS):
        place = lax.broadcasted_iota(jnp.int32, (padded, lanes), 1) + tile * lanes
        picked = jnp.take_along_axis(table, place // OFFSETS, axis=1)
        sums = []
        for channel in range(owned):
            mask = row_index == (place % OFFSETS) * owned + channel
            sums.append(jnp.sum(jnp.where(mask, picked, 0.0), axis=0, keepdims=True))
        tiles.append(jnp.concatenate(sums, axis=0))
    return jnp.concatenate(tiles, axis=1)


def solve_body(scale, centered_ref, across_ref, *refs):
    *part_refs, update_ref, coeffs_ref = refs
    rows, total, lanes = centered_ref.shape
    samples = coeffs_ref.shape[1]
    summed = part_refs[0][...]
    for ref in part_refs[1:]:
        summed = summed + ref[...]
    matrix = unfold(summed)
    row_index = lax.broadcasted_iota(jnp.int32, (WIDTH, total), 0)
    lane_index = lax.broadcasted_iota(jnp.int32, (WIDTH, total), 1)
    regular = [
        matrix[first : first + WIDTH] + jnp.where(lane_index == row_index + first, reg_shift, 0.0)
        for first in range(0, total, WIDTH)
    ]
    energies = summed[total // 2 + 1 : total // 2 + 2]
    deviation = energies - jnp.sum(energies, axis=1, keepdims=True) / total
    coeffs = solve_symmetric(regular, deviation)

    position = lax.axis_index("samp")
    sample = lax.broadcasted_iota(jnp.int32, (total, lanes), 0)
    lane = lax.broadcasted_iota(jnp.int32, (total, lanes), 1)
    spread = jnp.broadcast_to(coeffs, (lanes, total)).T
    own = jnp.sum(jnp.where(sample == lane + position * samples, spread, 0.0), axis=0, keepdims=True)
    coeffs_ref[...] = own[:, :samples]

    spread = spread * scale
    own, across = (
        arrange([jnp.sum(ref[row].astype(F32) * spread, axis=0, keepdims=True) for row in range(rows)])
        for ref in (centered_ref, across_ref)
    )
    even = position % CORES == 0
    owned = own.shape[0]
    update_ref[0:owned, :] = jnp.where(even, own, across)
    update_ref[owned : 2 * owned, :] = jnp.where(even, across, own)


def far_first(members):
    return [*range(members // 2, members), *range(CORES, members // 2), *range(1, CORES)]


def swaps(x, axis, masks):
    return {mask: swap(x, axis, mask) for mask in sorted(masks, reverse=True)}


def in_order(x, axis, masks):
    blocks = {0: x, **swaps(x, axis, masks)}
    bits = lax.axis_index(axis) & functools.reduce(lambda a, b: a | b, masks)
    placed = []
    for place in sorted(blocks):
        block = blocks[0]
        for mask in sorted(masks):
            block = jnp.where(bits == place ^ mask, blocks[mask], block)
        placed.append(block)
    return jnp.concatenate(placed)


def solve_system(gram, dev_all, total):
    regular = gram + reg_shift * jnp.eye(total, dtype=F32)
    factor = jnp.linalg.cholesky(regular)
    forward = lax.linalg.triangular_solve(factor, dev_all[:, None], left_side=True, lower=True)
    return lax.linalg.triangular_solve(factor, forward, left_side=True, lower=True, transpose_a=True)[:, 0]


def local_split(activations, cotangents, energies):
    samples, layers, channels, sites = activations.shape
    owned = cotangents.shape[2]
    members = lax.axis_size("samp")
    chips = members // CORES
    total = members * samples
    position = lax.axis_index("samp")
    params_all = LAYERS * C * C * OFFSETS
    mine = owned // members
    rows = OFFSETS * mine

    own = jax.ShapeDtypeStruct((rows, samples, LANES), F32)
    block = jax.ShapeDtypeStruct((packed_rows(rows, samples), LANES), F32)
    inputs = [pltpu.with_memory_space_constraint(x, pltpu.HBM) for x in (activations, cotangents)]

    def half(far, out_shape):
        return kernel_call(
            functools.partial(grads_body, far),
            out_shape,
            [
                pltpu.VMEM(activations.shape, BF16),
                pltpu.VMEM(cotangents.shape, BF16),
                pltpu.VMEM((OFFSETS, samples * layers * owned // 2, sites), BF16),
                pltpu.VMEM(((OFFSETS * owned // 2 + 1) * samples, LANES), F32),
                pltpu.SemaphoreType.DMA((2,)),
            ],
            in_specs=[pl.BlockSpec(memory_space=pltpu.HBM)] * 2,
        )(*inputs)

    far_blocks = half(True, (block,) * (members // 2))
    own, *near_blocks = half(False, (own,) + (block,) * (members // 2 - 1))
    blocks = [*near_blocks, *far_blocks]
    order = far_first(members)
    arrived = [swap(blocks[slot - 1].astype(jnp.float16), "samp", slot).astype(F32) for slot in order]

    lane = jnp.arange(total) // samples
    here = (lane == position) & (lax.axis_index("par") == 0)
    spread = jnp.where(here, jnp.tile(energies, members), 0.0)
    spread = jnp.where(jnp.arange(8)[:, None] == 1, spread[None, :], 0.0)
    centered, partial_gram = kernel_call(
        functools.partial(gram_body, total, params_all),
        (jax.ShapeDtypeStruct((rows, total, LANES), BF16), jax.ShapeDtypeStruct((total // 2 + 8, total), F32)),
    )(spread, own, *arrived)

    summed = partial_gram + swap(partial_gram, "samp", 1)
    ready, summed = lax.optimization_barrier((centered, summed))
    across = swap(ready, "samp", 1)
    masks = [*range(2, lax.axis_size("par")), 1]
    summed = sum((swap(summed, "par", mask) for mask in masks), start=summed)
    parts = [summed, *swaps(summed, "samp", range(CORES, members, CORES)).values()]
    update, local_coeffs = kernel_call(
        functools.partial(solve_body, -math.sqrt(params_all / total)),
        (jax.ShapeDtypeStruct((CORES * mine, OFFSETS * LANES), F32), jax.ShapeDtypeStruct((1, samples), F32)),
    )(centered, across, *parts)
    update = in_order(update, "samp", range(CORES, members, CORES))
    return update, local_coeffs[0]


def local_gather(activations, cotangents, energies):
    samples, layers, channels, sites = activations.shape
    owned = cotangents.shape[2]
    position = lax.axis_index("samp")
    total = lax.axis_size("samp") * samples
    params_all = LAYERS * C * C * OFFSETS
    field = cotangents.reshape(samples, layers, owned, SIDE, SIDE)
    shifted = [jnp.roll(field, (row - 1, col - 1), axis=(3, 4)) for row in range(3) for col in range(3)]
    stacked = jnp.stack(shifted, axis=3).reshape(samples, layers, owned * OFFSETS, sites)
    grads = jnp.einsum("slkx,slix->slki", stacked, activations, preferred_element_type=F32)
    grads = grads.reshape(samples, layers, owned, OFFSETS, channels).transpose(0, 2, 1, 4, 3)
    grads = grads.reshape(samples, owned * layers * channels * OFFSETS)
    col_sums, energy_sum = lax.psum((jnp.sum(grads, axis=0), jnp.sum(energies)), "samp")
    centered = ((grads - col_sums / total) * (1.0 / math.sqrt(params_all))).astype(BF16)
    everyone = lax.all_gather(centered, "samp", axis=0, tiled=True)
    partial_gram = lax.dot_general(centered, everyone, (((1,), (1,)), ((), ())), preferred_element_type=F32)
    gram = lax.all_gather(lax.psum(partial_gram, "par"), "samp", axis=0, tiled=True)
    deviation = lax.all_gather(energies - energy_sum / total, "samp", axis=0, tiled=True)
    coeffs = solve_system(gram, deviation, total)
    local_coeffs = lax.dynamic_slice_in_dim(coeffs, position * samples, samples)
    term = jnp.dot(local_coeffs[None, :], centered.astype(F32), precision=lax.Precision.HIGHEST)[0]
    update = -math.sqrt(params_all / total) * lax.psum(term, "samp")
    return update.reshape(owned, -1), local_coeffs


def local(activations, cotangents, energies):
    if cotangents.shape[2] % lax.axis_size("samp"):
        return local_gather(activations, cotangents, energies)
    return local_split(activations, cotangents, energies)


def solution(mesh):
    return jax.shard_map(
        local,
        mesh=mesh,
        in_specs=(P("samp", None, None, None), P("samp", None, "par", None), P("samp")),
        out_specs=(P("par", None), P("samp")),
        check_vma=False,
    )
```

```python
import functools
import math

import jax
import jax.numpy as jnp
from jax import lax
from jax.experimental import pallas as pl
from jax.experimental.pallas import tpu as pltpu
from jax.sharding import PartitionSpec as P

C = 64
SIDE = 16
LAYERS = 2
SITES = SIDE * SIDE
OFFSETS = 9
LANES = 128
CORES = 2


reg_shift = 0.1
F32 = jnp.float32
BF16 = jnp.bfloat16
VMEM_LIMIT = 48 * 1024 * 1024


def kernel_call(body, out_shape, scratch_shapes=(), **options):
    return pl.pallas_call(
        body,
        out_shape=out_shape,
        **options,
        scratch_shapes=scratch_shapes,
        compiler_params=pltpu.CompilerParams(vmem_limit_bytes=VMEM_LIMIT),
    )


def swap(x, axis, mask):
    count = lax.axis_size(axis)
    return lax.ppermute(x, axis, [(i, i ^ mask) for i in range(count)])


def exponent(values):
    top = jnp.maximum(jnp.max(jnp.abs(values), axis=0, keepdims=True), 1e-30)
    return 14.0 - jnp.floor(jnp.log2(top))


def packed_rows(rows, samples):
    return -(-(rows * samples + rows + 2) // 8) * 8


def grads_body(far, acts_hbm, cots_hbm, *refs):
    *out_refs, acts_ref, cots_ref, shifted_ref, grads_ref, semaphores = refs
    copies = [
        pltpu.make_async_copy(cots_hbm, cots_ref, semaphores.at[0]),
        pltpu.make_async_copy(acts_hbm, acts_ref, semaphores.at[1]),
    ]
    for copy in copies:
        copy.start()
    samples, layers, owned, sites = cots_ref.shape
    members = len(out_refs)
    owned = owned // 2
    mine = owned // members
    rows = OFFSETS * mine
    moves = []
    source = lax.broadcasted_iota(jnp.int32, (sites, sites), 0)
    target = lax.broadcasted_iota(jnp.int32, (1, sites), 1)
    for offset in range(OFFSETS):
        row, col = target // SIDE, target % SIDE
        row = (row + SIDE - (offset // 3 - 1)) % SIDE
        col = (col + SIDE - (offset % 3 - 1)) % SIDE
        moves.append(jnp.where(source == row * SIDE + col, 1.0, 0.0).astype(BF16))
    position = lax.axis_index("samp")
    upper = (position // members + int(far)) % 2 == 1
    copies[0].wait()
    field = cots_ref[...].astype(F32).reshape(samples * layers, 2, owned, sites)
    field = jnp.where(upper, field[:, 1], field[:, 0]).reshape(samples * layers * owned, sites).astype(BF16)
    for offset in range(OFFSETS):
        shifted_ref[offset] = jnp.dot(field, moves[offset], preferred_element_type=F32).astype(BF16)
    copies[1].wait()
    lanes = grads_ref.shape[1]
    lane = lax.broadcasted_iota(jnp.int32, (OFFSETS, owned, lanes), 2)
    for sample in range(samples):
        first = sample * layers * owned
        left = jnp.concatenate([shifted_ref[k, first : first + layers * owned, :] for k in range(OFFSETS)], axis=0)
        right = acts_ref[sample].reshape(layers * C, sites)
        products = lax.dot_general(left, right, (((1,), (1,)), ((), ())), preferred_element_type=F32)
        products = products.reshape(OFFSETS, layers, owned, lanes)
        grads = products[:, 0]
        for layer in range(1, layers):
            grads = jnp.where(lane >= layer * C, products[:, layer], grads)
        grads_ref[pl.ds(sample, OFFSETS * owned, stride=samples), :] = grads.reshape(OFFSETS * owned, lanes)
    for index in range(members):
        slot = index + members * int(far)
        start = ((position ^ slot) % members) * (mine * samples)
        pieces = [
            grads_ref[pl.ds(pl.multiple_of(k * owned * samples + start, mine * samples), mine * samples), :] for k in range(OFFSETS)
        ]
        values = jnp.concatenate(pieces, axis=0).reshape(rows, samples, lanes)
        values_ref = out_refs[index]
        if slot == 0:
            values_ref[...] = values
            continue
        reference = (jnp.sum(values, axis=1) * (1.0 / samples)).astype(BF16).astype(F32)
        values = values - reference[:, None, :]
        shift = exponent(jnp.max(jnp.abs(values), axis=0))
        reference_shift = exponent(reference)
        last = rows * samples
        values_ref[0:last, :] = (values * jnp.exp2(shift)).reshape(last, lanes)
        values_ref[last : last + rows, :] = reference * jnp.exp2(reference_shift)
        values_ref[last + rows : last + rows + 1, :] = shift
        values_ref[last + rows + 1 : last + rows + 2, :] = reference_shift
        spare = values_ref.shape[0] - (last + rows + 2)
        if spare:
            values_ref[last + rows + 2 :, :] = jnp.zeros((spare, lanes), F32)


def halves(half):
    row = lax.broadcasted_iota(jnp.int32, (half, 2 * half), 0)
    lane = lax.broadcasted_iota(jnp.int32, (half, 2 * half), 1)
    return row, lane


def fold(matrix, energies):
    half = matrix.shape[0] // 2
    row, lane = halves(half)
    top, bottom = matrix[:half], matrix[half:]
    turned = pltpu.roll(bottom, half, 1)
    diagonal = jnp.sum(jnp.where(lane == row, turned, 0.0), axis=0, keepdims=True)
    first = lax.broadcasted_iota(jnp.int32, energies.shape, 0) == 0
    rest = jnp.where(first, diagonal, energies)
    return jnp.concatenate([jnp.where((lane > row) & (lane < half), turned, top), rest], axis=0)


def unfold(folded):
    half = folded.shape[1] // 2
    row, lane = halves(half)
    body, diagonal = folded[:half], folded[half : half + 1]
    flipped = body.T
    mixed, crossed = flipped[:half], flipped[half:]
    both = jnp.concatenate([mixed, crossed], axis=1)
    top = jnp.where((lane > row) & (lane < half), both, body)
    lower = jnp.concatenate([crossed, mixed], axis=1)
    turned = pltpu.roll(body, half, 1)
    place = lane - half
    corner = jnp.where(place > row, turned, jnp.where(place == row, pltpu.roll(jnp.broadcast_to(diagonal, turned.shape), half, 1), lower))
    return jnp.concatenate([top, jnp.where(lane < half, lower, corner)], axis=0)


def gram_body(total, params_all, energies_ref, own_ref, *refs):
    rows, group, lanes = own_ref.shape
    *value_refs, centered_ref, gram_ref = refs
    by_slot = dict(zip(far_first(len(value_refs) + 1), value_refs))
    value_refs = [by_slot[slot] for slot in sorted(by_slot)]
    position = lax.axis_index("samp")
    gram = jnp.zeros((total, total), F32)
    last = rows * group
    scales = [jnp.exp2(-ref[last + rows : last + rows + 1, :]) for ref in value_refs]
    references = [ref[last : last + rows, :] * jnp.exp2(-ref[last + rows + 1 : last + rows + 2, :]) for ref in value_refs]
    pair = []
    for row in range(rows):
        blocks = [own_ref[row]]
        for ref, scale, reference in zip(value_refs, scales, references):
            blocks.append(ref[row * group : (row + 1) * group, :] * scale + reference[row : row + 1, :])
        mean = sum(jnp.sum(block, axis=0, keepdims=True) for block in blocks) / total
        for slot in range(len(blocks)):
            place = pl.ds(pl.multiple_of((position ^ slot) * group, group), group)
            centered_ref[row, place, :] = ((blocks[slot] - mean) * (1.0 / math.sqrt(params_all))).astype(BF16)
        pair.append(centered_ref[row])
        if len(pair) == 2 or row == rows - 1:
            both = jnp.concatenate(pair, axis=1)
            gram = gram + lax.dot_general(both, both, (((1,), (1,)), ((), ())), preferred_element_type=F32)
            pair = []
    gram_ref[...] = fold(gram, energies_ref[...])


WIDTH = 16


def thirds(values):
    high = values.astype(BF16)
    rest = values - high.astype(F32)
    middle = rest.astype(BF16)
    return high, middle, (rest - middle.astype(F32)).astype(BF16)


def outer_sum(left, right):
    a, b, c = thirds(left)
    d, e, f = thirds(right)
    lefts = jnp.concatenate([a, a, b, a, b, c], axis=0)
    rights = jnp.concatenate([d, e, d, f, e, d], axis=0)
    return lax.dot_general(lefts, rights, (((0,), (0,)), ((), ())), preferred_element_type=F32)


def spread_lane(rows, lane):
    return jnp.broadcast_to(rows[:, lane : lane + 1], rows.shape)


def eliminate(block, panel, row):
    block = list(block)
    for step in range(0, len(block), 2):
        one, two = block[step], block[step + 1]
        a, b, c = one[step : step + 1], two[step : step + 1], two[step + 1 : step + 2]
        inverse = 1.0 / (a * c - b * b)
        upper_row, lower_row = row == step, row == step + 1
        done = upper_row | lower_row
        one = jnp.where(done, jnp.where(upper_row, -1.0, 0.0), one)
        two = jnp.where(done, jnp.where(lower_row, -1.0, 0.0), two)

        def reduced(rows):
            upper, lower = rows[step : step + 1], rows[step + 1 : step + 2]
            first, second = (c * upper - b * lower) * inverse, (a * lower - b * upper) * inverse
            return jnp.where(done, 0.0, rows) - (one * first + two * second)

        panel = reduced(panel)
        block = [reduced(rows) if c >= step + 2 else rows for c, rows in enumerate(block)]
    return panel


def as_column(values, rows, first):
    row = lax.broadcasted_iota(jnp.int32, (rows, values.shape[1]), 0)
    lane = lax.broadcasted_iota(jnp.int32, (rows, values.shape[1]), 1)
    return jnp.sum(jnp.where(lane == row + first, values, 0.0), axis=1, keepdims=True)


def solve_symmetric(matrix, right):
    matrix = list(matrix)
    count, size = len(matrix), WIDTH * len(matrix)
    row = lax.broadcasted_iota(jnp.int32, (WIDTH, size), 0)
    lane = lax.broadcasted_iota(jnp.int32, (WIDTH, size), 1)
    columns = [as_column(right, WIDTH, WIDTH * index) for index in range(count)]
    pivot = matrix[0]
    for index in range(count):
        first = WIDTH * index
        inside = (lane >= first) & (lane < first + WIDTH)
        unit = jnp.where(lane == row + first, 1.0, 0.0)
        solved = eliminate([spread_lane(pivot, first + c) for c in range(WIDTH)], jnp.where(inside, unit, pivot), row)
        solved = jnp.where(inside, -solved, solved)
        held = jnp.where(inside, 0.0, pivot)
        if index + 1 == count:
            weights = columns[index] - jnp.sum(held * right, axis=1, keepdims=True)
            terms = [jnp.where(inside, 0.0, matrix[other]) * columns[other] for other in range(index)]
            return -jnp.sum(sum(terms) + solved * weights, axis=0, keepdims=True)
        update = outer_sum(held, solved)
        following = jnp.where(inside, 0.0, matrix[index + 1])
        for c in range(WIDTH):
            following = following - spread_lane(matrix[index + 1], first + c) * solved[c : c + 1]
        for other in range(count):
            if other == index:
                matrix[other] = solved
            elif other == index + 1:
                matrix[other] = following
            else:
                matrix[other] = jnp.where(inside, 0.0, matrix[other]) - update[WIDTH * other : WIDTH * (other + 1)]
        pivot = following


def arrange(terms):
    rows, lanes = len(terms), terms[0].shape[1]
    owned = rows // OFFSETS
    padded = -(-rows // 8) * 8
    table = jnp.concatenate(terms + [jnp.zeros((padded - rows, lanes), F32)], axis=0)
    row_index = lax.broadcasted_iota(jnp.int32, (padded, lanes), 0)
    tiles = []
    for tile in range(OFFSETS):
        place = lax.broadcasted_iota(jnp.int32, (padded, lanes), 1) + tile * lanes
        picked = jnp.take_along_axis(table, place // OFFSETS, axis=1)
        sums = []
        for channel in range(owned):
            mask = row_index == (place % OFFSETS) * owned + channel
            sums.append(jnp.sum(jnp.where(mask, picked, 0.0), axis=0, keepdims=True))
        tiles.append(jnp.concatenate(sums, axis=0))
    return jnp.concatenate(tiles, axis=1)


def solve_body(scale, centered_ref, across_ref, *refs):
    *part_refs, update_ref, coeffs_ref = refs
    rows, total, lanes = centered_ref.shape
    samples = coeffs_ref.shape[1]
    summed = part_refs[0][...]
    for ref in part_refs[1:]:
        summed = summed + ref[...]
    matrix = unfold(summed)
    row_index = lax.broadcasted_iota(jnp.int32, (WIDTH, total), 0)
    lane_index = lax.broadcasted_iota(jnp.int32, (WIDTH, total), 1)
    regular = [
        matrix[first : first + WIDTH] + jnp.where(lane_index == row_index + first, reg_shift, 0.0)
        for first in range(0, total, WIDTH)
    ]
    energies = summed[total // 2 + 1 : total // 2 + 2]
    deviation = energies - jnp.sum(energies, axis=1, keepdims=True) / total
    coeffs = solve_symmetric(regular, deviation)

    position = lax.axis_index("samp")
    spread = jnp.broadcast_to(coeffs, (lanes, total)).T
    turned = pltpu.roll(jnp.broadcast_to(coeffs, (8, total)), (total - position * samples) % total, 1)
    coeffs_ref[...] = turned[:1, :samples]

    spread = spread * scale
    own, across = (
        arrange([jnp.sum(ref[row].astype(F32) * spread, axis=0, keepdims=True) for row in range(rows)])
        for ref in (centered_ref, across_ref)
    )
    even = position % CORES == 0
    owned = own.shape[0]
    update_ref[0:owned, :] = jnp.where(even, own, across)
    update_ref[owned : 2 * owned, :] = jnp.where(even, across, own)


def far_first(members):
    return [*range(members // 2, members), *range(CORES, members // 2), *range(1, CORES)]


def swaps(x, axis, masks):
    return {mask: swap(x, axis, mask) for mask in sorted(masks, reverse=True)}


def in_order(x, axis, masks):
    blocks = {0: x, **swaps(x, axis, masks)}
    bits = lax.axis_index(axis) & functools.reduce(lambda a, b: a | b, masks)
    placed = []
    for place in sorted(blocks):
        block = blocks[0]
        for mask in sorted(masks):
            block = jnp.where(bits == place ^ mask, blocks[mask], block)
        placed.append(block)
    return jnp.concatenate(placed)


def solve_system(gram, dev_all, total):
    regular = gram + reg_shift * jnp.eye(total, dtype=F32)
    factor = jnp.linalg.cholesky(regular)
    forward = lax.linalg.triangular_solve(factor, dev_all[:, None], left_side=True, lower=True)
    return lax.linalg.triangular_solve(factor, forward, left_side=True, lower=True, transpose_a=True)[:, 0]


def local_split(activations, cotangents, energies):
    samples, layers, channels, sites = activations.shape
    owned = cotangents.shape[2]
    members = lax.axis_size("samp")
    chips = members // CORES
    total = members * samples
    position = lax.axis_index("samp")
    params_all = LAYERS * C * C * OFFSETS
    mine = owned // members
    rows = OFFSETS * mine

    own = jax.ShapeDtypeStruct((rows, samples, LANES), F32)
    block = jax.ShapeDtypeStruct((packed_rows(rows, samples), LANES), F32)
    inputs = [pltpu.with_memory_space_constraint(x, pltpu.HBM) for x in (activations, cotangents)]

    def half(far, out_shape):
        return kernel_call(
            functools.partial(grads_body, far),
            out_shape,
            [
                pltpu.VMEM(activations.shape, BF16),
                pltpu.VMEM(cotangents.shape, BF16),
                pltpu.VMEM((OFFSETS, samples * layers * owned // 2, sites), BF16),
                pltpu.VMEM(((OFFSETS * owned // 2 + 1) * samples, LANES), F32),
                pltpu.SemaphoreType.DMA((2,)),
            ],
            in_specs=[pl.BlockSpec(memory_space=pltpu.HBM)] * 2,
        )(*inputs)

    far_blocks = half(True, (block,) * (members // 2))
    own, *near_blocks = half(False, (own,) + (block,) * (members // 2 - 1))
    blocks = [*near_blocks, *far_blocks]
    order = far_first(members)
    arrived = [swap(blocks[slot - 1].astype(jnp.float16), "samp", slot).astype(F32) for slot in order]

    lane = jnp.arange(total) // samples
    here = (lane == position) & (lax.axis_index("par") == 0)
    spread = jnp.where(here, jnp.tile(energies, members), 0.0)
    spread = jnp.where(jnp.arange(8)[:, None] == 1, spread[None, :], 0.0)
    centered, partial_gram = kernel_call(
        functools.partial(gram_body, total, params_all),
        (jax.ShapeDtypeStruct((rows, total, LANES), BF16), jax.ShapeDtypeStruct((total // 2 + 8, total), F32)),
    )(spread, own, *arrived)

    summed = partial_gram + swap(partial_gram, "samp", 1)
    ready, summed = lax.optimization_barrier((centered, summed))
    across = swap(ready, "samp", 1)
    masks = [*range(2, lax.axis_size("par")), 1]
    summed = sum((swap(summed, "par", mask) for mask in masks), start=summed)
    parts = [summed, *swaps(summed, "samp", range(CORES, members, CORES)).values()]
    update, local_coeffs = kernel_call(
        functools.partial(solve_body, -math.sqrt(params_all / total)),
        (jax.ShapeDtypeStruct((CORES * mine, OFFSETS * LANES), F32), jax.ShapeDtypeStruct((1, samples), F32)),
    )(centered, across, *parts)
    update = in_order(update, "samp", range(CORES, members, CORES))
    return update, local_coeffs[0]


def local_gather(activations, cotangents, energies):
    samples, layers, channels, sites = activations.shape
    owned = cotangents.shape[2]
    position = lax.axis_index("samp")
    total = lax.axis_size("samp") * samples
    params_all = LAYERS * C * C * OFFSETS
    field = cotangents.reshape(samples, layers, owned, SIDE, SIDE)
    shifted = [jnp.roll(field, (row - 1, col - 1), axis=(3, 4)) for row in range(3) for col in range(3)]
    stacked = jnp.stack(shifted, axis=3).reshape(samples, layers, owned * OFFSETS, sites)
    grads = jnp.einsum("slkx,slix->slki", stacked, activations, preferred_element_type=F32)
    grads = grads.reshape(samples, layers, owned, OFFSETS, channels).transpose(0, 2, 1, 4, 3)
    grads = grads.reshape(samples, owned * layers * channels * OFFSETS)
    col_sums, energy_sum = lax.psum((jnp.sum(grads, axis=0), jnp.sum(energies)), "samp")
    centered = ((grads - col_sums / total) * (1.0 / math.sqrt(params_all))).astype(BF16)
    everyone = lax.all_gather(centered, "samp", axis=0, tiled=True)
    partial_gram = lax.dot_general(centered, everyone, (((1,), (1,)), ((), ())), preferred_element_type=F32)
    gram = lax.all_gather(lax.psum(partial_gram, "par"), "samp", axis=0, tiled=True)
    deviation = lax.all_gather(energies - energy_sum / total, "samp", axis=0, tiled=True)
    coeffs = solve_system(gram, deviation, total)
    local_coeffs = lax.dynamic_slice_in_dim(coeffs, position * samples, samples)
    term = jnp.dot(local_coeffs[None, :], centered.astype(F32), precision=lax.Precision.HIGHEST)[0]
    update = -math.sqrt(params_all / total) * lax.psum(term, "samp")
    return update.reshape(owned, -1), local_coeffs


def local(activations, cotangents, energies):
    if cotangents.shape[2] % lax.axis_size("samp"):
        return local_gather(activations, cotangents, energies)
    return local_split(activations, cotangents, energies)


def solution(mesh):
    return jax.shard_map(
        local,
        mesh=mesh,
        in_specs=(P("samp", None, None, None), P("samp", None, "par", None), P("samp")),
        out_specs=(P("par", None), P("samp")),
        check_vma=False,
    )
```
